32 devices in a mesh: seq: 8 (over y, x, core), head: 4 (over z).
Axes of the slice: x: 2, y: 2, z: 4, core: 2. Of those that a mesh axis runs over, the one named last changes fastest.
Arguments:
- inputs: bfloat16 [32, 512, 768], P('seq'), may hold values from -6 to 6
- out_grad: bfloat16 [32, 512, 768], P('seq'), may hold values from -16 to 16
- w_query: bfloat16 [768, 512], P(None, 'head'), may hold values from -0.21875 to 0.21875
- w_key: bfloat16 [768, 512], P(None, 'head'), may hold values from -0.21875 to 0.21875
- w_value: bfloat16 [768, 512], P(None, 'head'), may hold values from -0.21875 to 0.21875
- w_output: bfloat16 [512, 768], P('head'), may hold values from -0.25 to 0.25
Outputs:
- grad_inputs: bfloat16 [32, 512, 768], P('seq', 'head')
- grad_wq: float32 [768, 512], P(None, 'head')
- grad_wk: float32 [768, 512], P(None, 'head')
- grad_wv: float32 [768, 512], P(None, 'head')
- grad_wo: float32 [512, 768], P('head')
The draws below stay inside these ranges and needn't reach their ends.
All inputs are finite; a program needn't handle non-finite values.
Results may differ from the reference program's by a relative error of at most 0.012.
Values may be sent and summed in bfloat16 or wider, within the bound.
No kernel may reach another device: no remote copies, remote signals or barrier semaphores. Data moves between devices by JAX's collectives and lax.ppermute only.
A program may use at most 64 MiB of HBM per device.

```python
import math
import jax
import jax.numpy as jnp
from jax import lax

D = 768
HEAD_DIM = 64
HEADS = 8
COLS = 512
ROWS = 32
TOKENS = 16384
HD = 512


def block_levels(own_key, extent, shards, low, high):
    gain = 1.0
    for dim, parts in shards:
        draws = jax.random.uniform(jax.random.fold_in(jax.random.fold_in(own_key, 6), dim), (parts,), jnp.float32, low / len(shards), high / len(shards))
        gain = gain * jnp.repeat(jnp.exp(draws), extent[dim] // parts).reshape((-1,) + (1,) * (len(extent) - 1 - dim))
    return gain


def bell_draw(key, extent, deviation, most, shards=(), held_as=jnp.bfloat16):
    array = jax.random.normal(key, extent, jnp.float32) * deviation
    if len(shards) > 0:
        array = block_levels(key, extent, shards, -0.22, 0.18) * array
    return jnp.clip(array, min=-most, max=most).astype(held_as)


def setup_inputs(seed: int = 0) -> dict:
    keys = jax.random.split(jax.random.key(seed), 7)
    inputs = bell_draw(keys[0], (ROWS, COLS, D), 1.0, 6.0, ((0, 8),))
    out_grad = bell_draw(keys[1], (ROWS, COLS, D), 4.0, 16.0, ((0, 8),))
    w_query = bell_draw(keys[2], (D, HD), D ** -0.5, 0.21875, ((1, 4),))
    w_key = bell_draw(keys[3], (D, HD), D ** -0.5, 0.21875, ((1, 4),))
    w_value = bell_draw(keys[4], (D, HD), D ** -0.5, 0.21875, ((1, 4),))
    w_output = bell_draw(keys[5], (HD, D), HD ** -0.5, 0.25, ((0, 4),))
    return {"inputs": inputs, "out_grad": out_grad, "w_query": w_query, "w_key": w_key, "w_value": w_value, "w_output": w_output}


def projected(source, matrix):
    flat = source.reshape(-1, source.shape[-1])
    return jnp.dot(flat, matrix, preferred_element_type=jnp.float32).astype(jnp.bfloat16)

def reference(inputs, out_grad, w_query, w_key, w_value, w_output):
    row_count, col_count, model_width = inputs.shape
    logit_scale = 1.0 / (math.sqrt(HEAD_DIM) * math.sqrt(ROWS))
    inv_root = 1.0 / math.sqrt(TOKENS)
    shape_heads = (row_count, col_count, HEADS, HEAD_DIM)
    query_proj = projected(inputs, w_query)
    key_proj = projected(inputs, w_key)
    value_proj = projected(inputs, w_value)
    query_four = query_proj.reshape(shape_heads).astype(jnp.float32)
    key_four = key_proj.reshape(shape_heads).astype(jnp.float32)
    value_four = value_proj.reshape(shape_heads).astype(jnp.float32)
    logits = logit_scale * jnp.einsum('rihe,rjhe->hij', query_four, key_four)
    exponent = jnp.exp(logits)
    attn_probs = exponent / lax.optimization_barrier(jnp.sum(exponent, axis=2, keepdims=True))
    probs_low = attn_probs.astype(jnp.bfloat16)
    attended = jnp.einsum('hij,rjhe->rihe', probs_low.astype(jnp.float32), value_four).astype(jnp.bfloat16)
    flat_in = inputs.reshape(-1, model_width)
    flat_grad = out_grad.reshape(-1, model_width)
    grad_wo = jnp.dot(attended.reshape(-1, HD).T, flat_grad, preferred_element_type=jnp.float32) * inv_root
    grad_att = jnp.dot(flat_grad, w_output.T, preferred_element_type=jnp.float32).astype(jnp.bfloat16)
    grad_four = grad_att.reshape(shape_heads).astype(jnp.float32)
    grad_probs = jnp.einsum('rihe,rjhe->hij', grad_four, value_four)
    row_inner = lax.optimization_barrier(jnp.sum(attn_probs * grad_probs, axis=2, keepdims=True))
    grad_logits = (logit_scale * attn_probs * (grad_probs - row_inner)).astype(jnp.bfloat16)
    logit_four = grad_logits.astype(jnp.float32)
    grad_value = jnp.einsum('hij,rihe->rjhe', probs_low.astype(jnp.float32), grad_four).astype(jnp.bfloat16)
    grad_query = jnp.einsum('hij,rjhe->rihe', logit_four, key_four).astype(jnp.bfloat16)
    grad_key = jnp.einsum('hij,rihe->rjhe', logit_four, query_four).astype(jnp.bfloat16)
    flat_q = grad_query.reshape(-1, HD)
    flat_k = grad_key.reshape(-1, HD)
    flat_v = grad_value.reshape(-1, HD)
    grad_flat = jnp.dot(flat_q, w_query.T, preferred_element_type=jnp.float32)
    grad_flat = grad_flat + jnp.dot(flat_k, w_key.T, preferred_element_type=jnp.float32)
    grad_flat = grad_flat + jnp.dot(flat_v, w_value.T, preferred_element_type=jnp.float32)
    grad_inputs = grad_flat.astype(jnp.bfloat16).reshape(row_count, col_count, model_width)
    grad_wq = jnp.dot(flat_in.T, flat_q, preferred_element_type=jnp.float32) * inv_root
    grad_wk = jnp.dot(flat_in.T, flat_k, preferred_element_type=jnp.float32) * inv_root
    grad_wv = jnp.dot(flat_in.T, flat_v, preferred_element_type=jnp.float32) * inv_root
    return (grad_inputs, grad_wq, grad_wk, grad_wv, grad_wo)
```

```python
import math
from functools import partial

import jax
import jax.numpy as jnp
from jax import lax
from jax.experimental import pallas as pl
from jax.experimental.pallas import tpu as pltpu
from jax.sharding import PartitionSpec as P

HEAD_DIM = 64
F32 = jnp.float32
BF16 = jnp.bfloat16
VMEM_BYTES = 40 * 1024 * 1024


def dot_nn(left, right):
    return lax.dot_general(left, right, (((1,), (0,)), ((), ())), preferred_element_type=F32)


def dot_nt(left, right):
    return lax.dot_general(left, right, (((1,), (1,)), ((), ())), preferred_element_type=F32)


def vmem_spec():
    return pl.BlockSpec(memory_space=pltpu.VMEM)


def smem_spec():
    return pl.BlockSpec(memory_space=pltpu.SMEM)


def call(kernel, outs, ins, scratch=(), flops=0, moved=0, name=None):
    return pl.pallas_call(
        kernel,
        out_shape=outs,
        in_specs=[smem_spec()] + [vmem_spec()] * (len(ins) - 1),
        out_specs=jax.tree.map(lambda _: vmem_spec(), outs),
        scratch_shapes=list(scratch),
        compiler_params=pltpu.CompilerParams(vmem_limit_bytes=VMEM_BYTES),
        cost_estimate=pl.CostEstimate(flops=flops, bytes_accessed=moved, transcendentals=0),
        name=name,
    )(*ins)


def front_kernel(place, x, og, wq, wk, wv, wo, wt, qt, kt, vt, gt, keep, give, qn, gn):
    step = pl.program_id(0)
    width = wq.shape[1]
    heads = width // HEAD_DIM
    pieces, piece_rows, _ = keep.shape
    cols = kt.shape[2]

    @pl.when(step == 0)
    def _():
        wt[0:width, :] = wq[...].T
        wt[width : 2 * width, :] = wk[...].T
        wt[2 * width : 3 * width, :] = wv[...].T

    three = dot_nt(wt[...], x[0]).astype(BF16)
    one = dot_nt(wo[...], og[0]).astype(BF16)
    rows = pl.ds(pl.multiple_of(step * HEAD_DIM, HEAD_DIM), HEAD_DIM)
    for h in range(heads):
        at = h * HEAD_DIM
        qt[h, rows, :] = three[at : at + HEAD_DIM]
        kt[h, rows, :] = three[width + at : width + at + HEAD_DIM]
        vt[h, rows, :] = three[2 * width + at : 2 * width + at + HEAD_DIM]
        gt[h, rows, :] = one[at : at + HEAD_DIM]

    @pl.when(step == pl.num_programs(0) - 1)
    def _():
        chip, core = place[0], place[1]
        for h in range(heads):
            qn[...] = qt[h].T
            gn[...] = gt[h].T
            for i in range(0, cols, piece_rows):
                shard = (h * cols + i) // piece_rows
                logits = dot_nn(qn[i : i + piece_rows, :], kt[h]).astype(BF16)
                probs = dot_nn(gn[i : i + piece_rows, :], vt[h]).astype(BF16)
                slot = jnp.bitwise_xor(chip, shard // 2)

                @pl.when(core == shard % 2)
                def _():
                    keep[slot, :, 0:cols] = logits
                    keep[slot, :, cols:] = probs

                @pl.when(core != shard % 2)
                def _():
                    give[slot, :, 0:cols] = logits
                    give[slot, :, cols:] = probs


def pair_kernel(place, keep, got, *outs):
    for k, out in enumerate(outs):
        out[...] = (keep[k].astype(F32) + got[k].astype(F32)).astype(out.dtype)


def score_kernel(logit_scale, place, *refs):
    *parts, out = refs
    cols = out.shape[1] // 2
    total = parts[0][...].astype(F32)
    for part in parts[1:]:
        total = total + part[...].astype(F32)
    exponent = jnp.exp(total[:, 0:cols] * logit_scale)
    probs = exponent / jnp.sum(exponent, axis=1, keepdims=True)
    grad = total[:, cols:]
    inner = jnp.sum(probs * grad, axis=1, keepdims=True)
    out[:, 0:cols] = probs.astype(BF16)
    out[:, cols:] = (logit_scale * probs * (grad - inner)).astype(BF16)


def grads_kernel(pieces, place, *refs):
    mine, other = refs[0:pieces], refs[pieces : 2 * pieces]
    qt, kt, vt, gt = refs[2 * pieces : 2 * pieces + 4]
    sends = refs[2 * pieces + 4 : -4]
    three, att, probs, grads = refs[-4:]
    heads, merged, cols = qt.shape
    rows = merged // HEAD_DIM
    width = heads * HEAD_DIM
    piece_rows = mine[0].shape[0]
    chip, core, zed = place[0], place[1], place[2]
    for k in range(pieces):
        base = 2 * jnp.bitwise_xor(chip, k)
        for side, part in ((core, mine[k]), (1 - core, other[k])):
            at = pl.ds(pl.multiple_of((base + side) * piece_rows, piece_rows), piece_rows)
            probs[at, :] = part[:, 0:cols]
            grads[at, :] = part[:, cols:]
    for h in range(heads):
        p = probs[h * cols : (h + 1) * cols, :]
        s = grads[h * cols : (h + 1) * cols, :]
        grad_q = dot_nt(kt[h], s).astype(BF16)
        grad_k = dot_nn(qt[h], s).astype(BF16)
        grad_v = dot_nn(gt[h], p).astype(BF16)
        attended = dot_nt(vt[h], p).astype(BF16)
        for r in range(rows):
            src = slice(r * HEAD_DIM, (r + 1) * HEAD_DIM)
            for t, value in enumerate((grad_q, grad_k, grad_v)):
                at = t * width + h * HEAD_DIM
                three[r, at : at + HEAD_DIM, :] = value[src]
            att[r, h * HEAD_DIM : (h + 1) * HEAD_DIM, :] = attended[src]
    block = cols // len(sends)
    for k, send in enumerate(sends):
        at = pl.multiple_of(jnp.bitwise_xor(zed, k) * block, block)
        for r in range(rows):
            send[:, r * block : (r + 1) * block] = three[r, :, pl.ds(at, block)]


def weights_kernel(place, x, og, three, att, keep, give, total):
    step = pl.program_id(0)
    depth = three.shape[1]
    pieces, piece_rows, _ = keep.shape

    @pl.when(step == 0)
    def _():
        total[...] = jnp.zeros_like(total)

    total[0:depth, :] += dot_nn(three[0], x[0])
    total[depth:, :] += dot_nn(att[0], og[0])

    @pl.when(step == pl.num_programs(0) - 1)
    def _():
        chip, core = place[0], place[1]
        for k in range(pieces):
            base = 2 * jnp.bitwise_xor(chip, k)
            mine = pl.ds(pl.multiple_of((base + core) * piece_rows, piece_rows), piece_rows)
            other = pl.ds(pl.multiple_of((base + 1 - core) * piece_rows, piece_rows), piece_rows)
            keep[k] = total[mine, :].astype(BF16)
            give[k] = total[other, :].astype(BF16)


def sum_kernel(scale, place, *refs):
    *parts, out = refs
    total = parts[0][...].astype(F32)
    for part in parts[1:]:
        total = total + part[...].astype(F32)
    out[...] = (total * scale).astype(out.dtype)


def unpack_kernel(pieces, place, *refs):
    mine, other = refs[0:pieces], refs[pieces : 2 * pieces]
    outs, full = refs[2 * pieces : -1], refs[-1]
    piece_rows = mine[0].shape[0]
    chip, core = place[0], place[1]
    for k in range(pieces):
        base = 2 * jnp.bitwise_xor(chip, k)
        for side, part in ((core, mine[k]), (1 - core, other[k])):
            at = pl.ds(pl.multiple_of((base + side) * piece_rows, piece_rows), piece_rows)
            full[at, :] = part[...].astype(F32)
    width = full.shape[0] // len(outs)
    for t, out in enumerate(outs[:-1]):
        out[...] = full[t * width : (t + 1) * width, :].T
    outs[-1][...] = full[(len(outs) - 1) * width :, :]


def inputs_kernel(count, place, *refs):
    sent = refs[0:count]
    mine, other = refs[count : 2 * count], refs[2 * count : 3 * count]
    out = refs[-1]
    rows, block, model = out.shape
    half = model // 2
    core = place[1]
    lefts = [part[...].T for part in sent]
    for side, parts in ((core, mine), (1 - core, other)):
        total = dot_nn(lefts[0], parts[0][...])
        for left, part in zip(lefts[1:], parts[1:]):
            total = total + dot_nn(left, part[...])
        total = total.astype(BF16)
        at = pl.ds(pl.multiple_of(side * half, 128), half)
        for r in range(rows):
            out[r, :, at] = total[r * block : (r + 1) * block]


def body(inputs, out_grad, w_query, w_key, w_value, w_output):
    rows, cols, model = inputs.shape
    width = w_query.shape[1]
    heads = width // HEAD_DIM
    merged = rows * HEAD_DIM
    seqs, zeds = lax.axis_size("seq"), lax.axis_size("head")
    pieces = seqs // 2
    all_rows = rows * seqs
    logit_scale = 1.0 / (math.sqrt(HEAD_DIM) * math.sqrt(all_rows))
    inv_root = 1.0 / math.sqrt(all_rows * cols)
    shard = heads * cols // seqs
    wide = 4 * width // seqs
    me = lax.axis_index("seq")
    zed = lax.axis_index("head")
    place = jnp.stack([me // 2, me % 2, zed]).astype(jnp.int32)

    def swap(value):
        return lax.ppermute(value, "seq", [(i, i ^ 1) for i in range(seqs)])

    def across(value, k):
        return lax.ppermute(value, "seq", [(i, i ^ (2 * k)) for i in range(seqs)])

    def along(value, k):
        return lax.ppermute(value, "head", [(i, i ^ k) for i in range(zeds)])

    def shape(*dims, dtype=BF16):
        return jax.ShapeDtypeStruct(dims, dtype)

    whole = lambda *dims: pl.BlockSpec(dims, lambda r: (0,) * len(dims))
    row = pl.BlockSpec((1, cols, model), lambda r: (r, 0, 0))
    wt, qt, kt, vt, gt, keep, give = pl.pallas_call(
        front_kernel,
        grid=(rows,),
        out_shape=(
            shape(3 * width, model),
            shape(heads, merged, cols),
            shape(heads, merged, cols),
            shape(heads, merged, cols),
            shape(heads, merged, cols),
            shape(pieces, shard, 2 * cols),
            shape(pieces, shard, 2 * cols),
        ),
        in_specs=[smem_spec(), row, row]
        + [whole(model, width)] * 3
        + [whole(width, model)],
        out_specs=[whole(3 * width, model)]
        + [whole(heads, merged, cols)] * 4
        + [whole(pieces, shard, 2 * cols)] * 2,
        scratch_shapes=[pltpu.VMEM((cols, merged), BF16)] * 2,
        compiler_params=pltpu.CompilerParams(vmem_limit_bytes=VMEM_BYTES),
        name="front",
    )(place, inputs, out_grad, w_query, w_key, w_value, w_output)

    half = model // 2
    my_half = lax.dynamic_slice_in_dim(wt, (me % 2) * half, half, axis=1)
    mine_w = [my_half] + [along(my_half, k) for k in range(1, zeds)]
    other_w = [swap(value) for value in mine_w]

    got = swap(give)
    paired = call(
        pair_kernel, [shape(shard, 2 * cols)] * pieces, (place, keep, got), name="pair"
    )
    parts = [paired[0]] + [across(paired[k], k) for k in range(1, pieces)]
    scored = call(
        partial(score_kernel, logit_scale), shape(shard, 2 * cols), (place, *parts), name="score"
    )
    mine = [scored] + [across(scored, k) for k in range(1, pieces)]
    other = [swap(value) for value in mine]

    block = cols // zeds
    *sends, three, att = call(
        partial(grads_kernel, pieces),
        [shape(3 * width, rows * block)] * zeds
        + [shape(rows, 3 * width, cols), shape(rows, width, cols)],
        (place, *mine, *other, qt, kt, vt, gt),
        scratch=[pltpu.VMEM((heads * cols, cols), BF16)] * 2,
        name="grads",
    )
    sent = [sends[0]] + [along(sends[k], k) for k in range(1, zeds)]

    keep_w, give_w = pl.pallas_call(
        weights_kernel,
        grid=(rows,),
        out_shape=(shape(pieces, wide, model), shape(pieces, wide, model)),
        in_specs=[
            smem_spec(),
            row,
            row,
            pl.BlockSpec((1, 3 * width, cols), lambda r: (r, 0, 0)),
            pl.BlockSpec((1, width, cols), lambda r: (r, 0, 0)),
        ],
        out_specs=[whole(pieces, wide, model)] * 2,
        scratch_shapes=[pltpu.VMEM((4 * width, model), F32)],
        compiler_params=pltpu.CompilerParams(vmem_limit_bytes=VMEM_BYTES),
        name="weights",
    )(place, inputs, out_grad, three, att)
    got_w = swap(give_w)
    paired_w = call(
        pair_kernel, [shape(wide, model)] * pieces, (place, keep_w, got_w), name="pair_w"
    )
    parts_w = [paired_w[0]] + [across(paired_w[k], k) for k in range(1, pieces)]
    summed = call(partial(sum_kernel, inv_root), shape(wide, model), (place, *parts_w), name="sum_w")
    mine_g = [summed] + [across(summed, k) for k in range(1, pieces)]
    other_g = [swap(value) for value in mine_g]
    grad_q, grad_k, grad_v, grad_o = call(
        partial(unpack_kernel, pieces),
        [shape(model, width, dtype=F32)] * 3 + [shape(width, model, dtype=F32)],
        (place, *mine_g, *other_g),
        scratch=[pltpu.VMEM((4 * width, model), F32)],
        name="unpack",
    )
    grad_inputs = call(
        partial(inputs_kernel, zeds),
        shape(rows, block, model),
        (place, *sent, *mine_w, *other_w),
        name="inputs",
    )
    return (grad_inputs, grad_q, grad_k, grad_v, grad_o)


def solution(mesh):
    return jax.shard_map(
        body,
        mesh=mesh,
        in_specs=(
            P("seq", None, None),
            P("seq", None, None),
            P(None, "head"),
            P(None, "head"),
            P(None, "head"),
            P("head", None),
        ),
        out_specs=(
            P("seq", "head", None),
            P(None, "head"),
            P(None, "head"),
            P(None, "head"),
            P("head", None),
        ),
        check_vma=False,
    )
```

```python
import math
from functools import partial

import jax
import jax.numpy as jnp
from jax import lax
from jax.experimental import pallas as pl
from jax.experimental.pallas import tpu as pltpu
from jax.sharding import PartitionSpec as P

HEAD_DIM = 64
F32 = jnp.float32
BF16 = jnp.bfloat16
VMEM_BYTES = 16 * 1024 * 1024
SHARERS = 4


def dot_nn(left, right):
    return lax.dot_general(left, right, (((1,), (0,)), ((), ())), preferred_element_type=F32)


def dot_nt(left, right):
    return lax.dot_general(left, right, (((1,), (1,)), ((), ())), preferred_element_type=F32)


def vmem_spec():
    return pl.BlockSpec(memory_space=pltpu.VMEM)


def smem_spec():
    return pl.BlockSpec(memory_space=pltpu.SMEM)


def hbm_spec():
    return pl.BlockSpec(memory_space=pltpu.HBM)


def any_spec():
    return pl.BlockSpec(memory_space=pl.ANY)


def call(kernel, outs, ins, hbm=0, held=(), out_specs=None, scratch=(), flops=0, moved=0, name=None):
    count = len(ins)

    def run(*refs):
        kernel(*refs[:count], *refs[count + len(held) :])

    place, far, near = ins[0], ins[1 : 1 + hbm], ins[1 + hbm :]
    return pl.pallas_call(
        run,
        out_shape=outs,
        in_specs=[smem_spec()]
        + [hbm_spec()] * len(far)
        + [vmem_spec()] * len(near)
        + [any_spec()] * len(held),
        out_specs=out_specs or jax.tree.map(lambda _: vmem_spec(), outs),
        scratch_shapes=list(scratch),
        compiler_params=pltpu.CompilerParams(vmem_limit_bytes=VMEM_BYTES),
        cost_estimate=pl.CostEstimate(flops=flops, bytes_accessed=moved, transcendentals=0),
        name=name,
    )(place, *[far_array(x) for x in far], *near, *held)


def far_array(x):
    return pltpu.with_memory_space_constraint(x, pltpu.HBM)


def fetch(pairs, sems):
    copies = [pltpu.make_async_copy(src, dst, sems.at[i]) for i, (src, dst) in enumerate(pairs)]
    for copy in copies:
        copy.start()
    return copies


def deal(chip, core, shard, keep, give, value, first=0):
    slot = jnp.bitwise_xor(chip, shard // 2)

    cols = pl.ds(first, value.shape[1])

    @pl.when(core == shard % 2)
    def _():
        keep[slot, :, cols] = value

    @pl.when(core != shard % 2)
    def _():
        give[slot, :, cols] = value


def scores(chip, core, left, right, turned, keep, give, first):
    heads, _, cols = left.shape
    piece_rows = keep.shape[1]
    for h in range(heads):
        turned[...] = left[h].T
        total = dot_nn(turned[...], right[h]).astype(BF16)
        for i in range(0, cols, piece_rows):
            deal(chip, core, (h * cols + i) // piece_rows, keep, give, total[i : i + piece_rows], first)


def front_kernel(
    place, x, og, wq, wk, wv, wo, qt, kt, vt, gt, keep, give, slab,
    rows_x, rows_og, three_w, held_wo, both, turned, sems,
):
    rows = x.shape[0]
    width = wq.shape[1]
    loads = [pltpu.make_async_copy(w, three_w.at[t], sems.at[2, t]) for t, w in enumerate((wq, wk, wv))]
    loads.append(pltpu.make_async_copy(wo, held_wo, sems.at[2, 3]))
    in_x = [pltpu.make_async_copy(x.at[r], rows_x.at[r], sems.at[0, r]) for r in range(rows)]
    in_og = [pltpu.make_async_copy(og.at[r], rows_og.at[r], sems.at[1, r]) for r in range(rows)]
    for copy in loads + in_x + in_og:
        copy.start()
    for copy in loads:
        copy.wait()
    depth = slab.shape[0]
    at = pl.ds(pl.multiple_of(place[3] * depth, depth), depth)
    for t in range(3):
        both[t * width : (t + 1) * width, :] = three_w[t].T
        slab[:, t * width : (t + 1) * width] = three_w[t, at, :]
    for r in range(rows):
        in_x[r].wait()
        three = dot_nt(both[...], rows_x[r]).astype(BF16)
        at = slice(r * HEAD_DIM, (r + 1) * HEAD_DIM)
        for t, out in enumerate((qt, kt, vt)):
            for h in range(width // HEAD_DIM):
                first = t * width + h * HEAD_DIM
                out[h, at, :] = three[first : first + HEAD_DIM]
    scores(place[0], place[1], qt, kt, turned, keep, give, 0)
    for r in range(rows):
        in_og[r].wait()
        grad = dot_nt(held_wo[...], rows_og[r]).astype(BF16)
        at = slice(r * HEAD_DIM, (r + 1) * HEAD_DIM)
        for h in range(width // HEAD_DIM):
            gt[h, at, :] = grad[h * HEAD_DIM : (h + 1) * HEAD_DIM]
    scores(place[0], place[1], gt, vt, turned, keep, give, kt.shape[2])


def pair_kernel(place, keep, got, *outs):
    for k in range(keep.shape[0]):
        outs[k][...] = (keep[k].astype(F32) + got[k].astype(F32)).astype(outs[k].dtype)


def pair_pass_kernel(place, keep, got, slab, *outs):
    pair_kernel(place, keep, got, *outs[:-1])
    outs[-1][...] = slab[...]


def added(parts, cols=slice(None)):
    total = parts[0][:, cols].astype(F32)
    for part in parts[1:]:
        total = total + part[:, cols].astype(F32)
    return total


def score_kernel(logit_scale, place, *refs):
    *parts, out = refs
    cols = out.shape[1] // 2
    exponent = jnp.exp(added(parts, slice(0, cols)) * logit_scale)
    probs = exponent / jnp.sum(exponent, axis=1, keepdims=True)
    out[:, 0:cols] = probs.astype(BF16)
    grad = added(parts, slice(cols, None))
    inner = jnp.sum(probs * grad, axis=1, keepdims=True)
    out[:, cols:] = (logit_scale * probs * (grad - inner)).astype(BF16)


def assemble(place, mine, other, full):
    piece_rows = mine[0].shape[0]
    for k in range(len(mine)):
        base = 2 * jnp.bitwise_xor(place[0], k)
        for side, part in ((place[1], mine[k]), (1 - place[1], other[k])):
            at = pl.ds(pl.multiple_of((base + side) * piece_rows, piece_rows), piece_rows)
            full[at, :] = part[...].astype(full.dtype)


def grads_kernel(pieces, zeds, place, *refs):
    mine, other = refs[0:pieces], refs[pieces : 2 * pieces]
    qt, kt, vt, gt = refs[2 * pieces : 2 * pieces + 4]
    slabs = refs[2 * pieces + 4 : 2 * pieces + 3 + zeds]
    send_far, four_far, packed, full, send, four, sems = refs[2 * pieces + 3 + zeds :]
    heads, _, cols = qt.shape
    rows, stacked, _ = four.shape
    width = stacked // 4
    block = cols // zeds
    assemble(place, mine, other, full)
    for h in range(heads):
        span = slice(h * cols, (h + 1) * cols)
        values = (
            dot_nt(kt[h], full[span, cols:]),
            dot_nn(qt[h], full[span, cols:]),
            dot_nn(gt[h], full[span, 0:cols]),
            dot_nt(vt[h], full[span, 0:cols]),
        )
        for t, value in enumerate(values):
            value = value.astype(BF16)
            at = slice(t * width + h * HEAD_DIM, t * width + (h + 1) * HEAD_DIM)
            for r in range(rows):
                four[r, at, :] = value[r * HEAD_DIM : (r + 1) * HEAD_DIM]
    copies = []
    for z in range(zeds):
        for r in range(rows):
            part = four[r, 0 : 3 * width, z * block : (z + 1) * block]
            send[z, :, r * block : (r + 1) * block] = part
        copies += fetch([(send.at[z], send_far.at[z])], sems.at[pl.ds(z, 1)])
    copies += fetch([(four, four_far)], sems.at[pl.ds(zeds, 1)])
    for k, slab in enumerate(slabs):
        packed[k] = slab[...]
    for copy in copies:
        copy.wait()


def weights_kernel(place, x_far, og_far, four_far, keep, give, x, og, four, total, sems):
    rows, stacked, _ = four.shape
    three = 3 * stacked // 4
    piece_rows = keep.shape[1]
    copies = [
        fetch([(four_far.at[r], four.at[r]), (x_far.at[r], x.at[r]), (og_far.at[r], og.at[r])], sems.at[r])
        for r in range(rows)
    ]
    for r in range(rows):
        for copy in copies[r]:
            copy.wait()
        upper = dot_nn(four[r, 0:three, :], x[r])
        lower = dot_nn(four[r, three:, :], og[r])
        if r == 0:
            total[0:three, :] = upper
            total[three:, :] = lower
        else:
            total[0:three, :] += upper
            total[three:, :] += lower
    for i in range(0, stacked, piece_rows):
        value = total[i : i + piece_rows, :].astype(BF16)
        deal(place[0], place[1], i // piece_rows, keep, give, value)


def sum_kernel(scale, place, *refs):
    *parts, out = refs
    out[...] = (added(parts) * scale).astype(out.dtype)


def unpack_kernel(pieces, place, *refs):
    mine, other = refs[0:pieces], refs[pieces : 2 * pieces]
    outs, full = refs[2 * pieces : -1], refs[-1]
    assemble(place, mine, other, full)
    width = full.shape[0] // len(outs)
    for t, out in enumerate(outs[:-1]):
        out[...] = full[t * width : (t + 1) * width, :].T
    outs[-1][...] = full[(len(outs) - 1) * width :, :]


def gather_weights_kernel(slabs, place, wq, wk, wv, *refs):
    mine, other, full = refs[0:slabs], refs[slabs : 2 * slabs], refs[-1]
    zeds, _, _ = full.shape
    width = wq.shape[1]
    depth = mine[0].shape[1]
    zed = place[2]
    for t, own in enumerate((wq, wk, wv)):
        full[zed, :, t * width : (t + 1) * width] = own[...]
    for k in range(slabs):
        base = 2 * jnp.bitwise_xor(place[3] // 2, k)
        for side, part in ((place[1], mine[k]), (1 - place[1], other[k])):
            at = pl.ds(pl.multiple_of((base + side) * depth, depth), depth)
            for z in range(1, zeds):
                full[jnp.bitwise_xor(zed, z), at, :] = part[z - 1]


def inputs_kernel(place, sent_far, full, out, sent, sems):
    rows, block, _ = out.shape
    zeds = sent.shape[0]
    copies = fetch([(sent_far.at[z], sent.at[z]) for z in range(zeds)], sems)
    copies[0].wait()
    value = dot_nt(sent[0].T, full[0])
    for z in range(1, zeds):
        copies[z].wait()
        value = value + dot_nt(sent[z].T, full[z])
    value = value.astype(BF16)
    for r in range(rows):
        out[r] = value[r * block : (r + 1) * block]


def body(inputs, out_grad, w_query, w_key, w_value, w_output):
    rows, cols, model = inputs.shape
    width = w_query.shape[1]
    heads = width // HEAD_DIM
    merged = rows * HEAD_DIM
    seqs, zeds = lax.axis_size("seq"), lax.axis_size("head")
    pieces = seqs // 2
    all_rows = rows * seqs
    logit_scale = 1.0 / (math.sqrt(HEAD_DIM) * math.sqrt(all_rows))
    inv_root = 1.0 / math.sqrt(all_rows * cols)
    shard = heads * cols // seqs
    wide = 4 * width // seqs
    block = cols // zeds
    sharers = min(seqs, SHARERS)
    depth = model // sharers
    me = lax.axis_index("seq")
    zed = lax.axis_index("head")
    place = jnp.stack([me // 2, me % 2, zed, me % sharers]).astype(jnp.int32)

    def swap(value):
        return lax.ppermute(value, "seq", [(i, i ^ 1) for i in range(seqs)])

    def across(value, k):
        return lax.ppermute(value, "seq", [(i, i ^ (2 * k)) for i in range(seqs)])

    def along(value, k):
        return lax.ppermute(value, "head", [(i, i ^ k) for i in range(zeds)])

    def shape(*dims, dtype=BF16):
        return jax.ShapeDtypeStruct(dims, dtype)

    def spread(paired):
        return [paired[0]] + [across(paired[k], k) for k in range(1, pieces)]

    def gathered(value, count):
        mine = [value] + [across(value, k) for k in range(1, count)]
        return mine, [swap(part) for part in mine]

    blocks = shape(heads, merged, cols)
    dealt = shape(pieces, shard, 2 * cols)
    rows_in = pltpu.VMEM((rows, cols, model), BF16)
    dot_flops = 2 * rows * cols * width * model
    score_flops = 2 * heads * cols * cols * merged

    qt, kt, vt, gt, keep, give, slab = call(
        front_kernel,
        (blocks,) * 4 + (dealt,) * 2 + (shape(depth, 3 * width),),
        (place, inputs, out_grad, w_query, w_key, w_value, w_output),
        hbm=6,
        scratch=[
            rows_in,
            rows_in,
            pltpu.VMEM((3, model, width), BF16),
            pltpu.VMEM((width, model), BF16),
            pltpu.VMEM((3 * width, model), BF16),
            pltpu.VMEM((cols, merged), BF16),
            pltpu.SemaphoreType.DMA((3, max(4, rows))),
        ],
        flops=4 * dot_flops + 2 * score_flops,
        name="front",
    )
    *paired, slab = call(
        pair_pass_kernel,
        [shape(shard, 2 * cols)] * pieces + [shape(*slab.shape)],
        (place, keep, swap(give), slab),
        name="pair_scores",
    )
    parts = spread(paired)
    slabs = [along(slab, k) for k in range(1, zeds)]
    scored = call(
        partial(score_kernel, logit_scale),
        shape(shard, 2 * cols),
        (place, *parts),
        held=slabs,
        name="score",
    )
    mine, other = gathered(scored, pieces)
    send, four, packed = call(
        partial(grads_kernel, pieces, zeds),
        (
            shape(zeds, 3 * width, rows * block),
            shape(rows, 4 * width, cols),
            shape(zeds - 1, depth, 3 * width),
        ),
        (place, *mine, *other, qt, kt, vt, gt, *slabs),
        out_specs=(hbm_spec(), hbm_spec(), vmem_spec()),
        scratch=[
            pltpu.VMEM((heads * cols, 2 * cols), BF16),
            pltpu.VMEM((zeds, 3 * width, rows * block), BF16),
            pltpu.VMEM((rows, 4 * width, cols), BF16),
            pltpu.SemaphoreType.DMA((zeds + 1,)),
        ],
        flops=4 * score_flops,
        name="grads",
    )
    sent = lax.all_to_all(send, "head", 0, 0, tiled=True)
    mine_w, other_w = gathered(packed, sharers // 2)

    keep, give = call(
        weights_kernel,
        [shape(pieces, wide, model)] * 2,
        (place, inputs, out_grad, four),
        hbm=3,
        scratch=[
            rows_in,
            rows_in,
            pltpu.VMEM((rows, 4 * width, cols), BF16),
            pltpu.VMEM((4 * width, model), F32),
            pltpu.SemaphoreType.DMA((rows, 3)),
        ],
        flops=4 * dot_flops,
        moved=inputs.size * 4,
        name="weights",
    )
    paired = call(
        pair_kernel, [shape(wide, model)] * pieces, (place, keep, swap(give)), name="pair_weights"
    )
    parts = spread(paired)
    full = call(
        partial(gather_weights_kernel, sharers // 2),
        shape(zeds, model, 3 * width),
        (place, w_query, w_key, w_value, *mine_w, *other_w),
        name="gather_weights",
    )
    total_w = call(
        partial(sum_kernel, inv_root),
        shape(wide, model),
        (place, *parts),
        held=(full,),
        name="sum_weights",
    )
    mine, other = gathered(total_w, pieces)
    grad_q, grad_k, grad_v, grad_o = call(
        partial(unpack_kernel, pieces),
        [shape(model, width, dtype=F32)] * 3 + [shape(width, model, dtype=F32)],
        (place, *mine, *other),
        scratch=[pltpu.VMEM((4 * width, model), F32)],
        name="unpack",
    )
    grad_inputs = call(
        inputs_kernel,
        shape(rows, block, model),
        (place, sent, full),
        hbm=1,
        scratch=[pltpu.VMEM((zeds, 3 * width, rows * block), BF16), pltpu.SemaphoreType.DMA((zeds,))],
        flops=3 * dot_flops,
        name="inputs",
    )
    return (grad_inputs, grad_q, grad_k, grad_v, grad_o)


def solution(mesh):
    return jax.shard_map(
        body,
        mesh=mesh,
        in_specs=(
            P("seq", None, None),
            P("seq", None, None),
            P(None, "head"),
            P(None, "head"),
            P(None, "head"),
            P("head", None),
        ),
        out_specs=(
            P("seq", "head", None),
            P(None, "head"),
            P(None, "head"),
            P(None, "head"),
            P("head", None),
        ),
        check_vma=False,
    )
```

```python
import math
from functools import partial

import jax
import jax.numpy as jnp
from jax import lax
from jax.experimental import pallas as pl
from jax.experimental.pallas import tpu as pltpu
from jax.sharding import PartitionSpec as P

HEAD_DIM = 64
F32 = jnp.float32
BF16 = jnp.bfloat16
VMEM_BYTES = 16 * 1024 * 1024
SHARERS = 8


def dot_nn(left, right):
    return lax.dot_general(left, right, (((1,), (0,)), ((), ())), preferred_element_type=F32)


def dot_nt(left, right):
    return lax.dot_general(left, right, (((1,), (1,)), ((), ())), preferred_element_type=F32)


def vmem_spec():
    return pl.BlockSpec(memory_space=pltpu.VMEM)


def smem_spec():
    return pl.BlockSpec(memory_space=pltpu.SMEM)


def hbm_spec():
    return pl.BlockSpec(memory_space=pltpu.HBM)


def any_spec():
    return pl.BlockSpec(memory_space=pl.ANY)


def call(kernel, outs, ins, hbm=0, held=(), out_specs=None, scratch=(), flops=0, moved=0, name=None):
    count = len(ins)

    def run(*refs):
        kernel(*refs[:count], *refs[count + len(held) :])

    place, far, near = ins[0], ins[1 : 1 + hbm], ins[1 + hbm :]
    return pl.pallas_call(
        run,
        out_shape=outs,
        in_specs=[smem_spec()]
        + [hbm_spec()] * len(far)
        + [vmem_spec()] * len(near)
        + [any_spec()] * len(held),
        out_specs=out_specs or jax.tree.map(lambda _: vmem_spec(), outs),
        scratch_shapes=list(scratch),
        compiler_params=pltpu.CompilerParams(vmem_limit_bytes=VMEM_BYTES),
        cost_estimate=pl.CostEstimate(flops=flops, bytes_accessed=moved, transcendentals=0),
        name=name,
    )(place, *[far_array(x) for x in far], *near, *held)


def far_array(x):
    return pltpu.with_memory_space_constraint(x, pltpu.HBM)


def fetch(pairs, sems):
    copies = [pltpu.make_async_copy(src, dst, sems.at[i]) for i, (src, dst) in enumerate(pairs)]
    for copy in copies:
        copy.start()
    return copies


def deal(chip, core, shard, keep, give, value, first=0):
    slot = jnp.bitwise_xor(chip, shard // 2)

    cols = pl.ds(first, value.shape[1])

    @pl.when(core == shard % 2)
    def _():
        keep[slot, :, cols] = value

    @pl.when(core != shard % 2)
    def _():
        give[slot, :, cols] = value


def scores(chip, core, left, right, turned, keep, give, first):
    heads, _, cols = left.shape
    piece_rows = keep.shape[1]
    for h in range(heads):
        turned[...] = left[h].T
        total = dot_nn(turned[...], right[h]).astype(BF16)
        for i in range(0, cols, piece_rows):
            deal(chip, core, (h * cols + i) // piece_rows, keep, give, total[i : i + piece_rows], first)


def front_kernel(
    place, x, og, wq, wk, wv, wo, qt, kt, vt, gt, keep, give, slab,
    rows_x, rows_og, three_w, held_wo, both, turned, sems,
):
    rows = x.shape[0]
    width = wq.shape[1]
    loads = [pltpu.make_async_copy(w, three_w.at[t], sems.at[2, t]) for t, w in enumerate((wq, wk, wv))]
    loads.append(pltpu.make_async_copy(wo, held_wo, sems.at[2, 3]))
    in_x = [pltpu.make_async_copy(x.at[r], rows_x.at[r], sems.at[0, r]) for r in range(rows)]
    in_og = [pltpu.make_async_copy(og.at[r], rows_og.at[r], sems.at[1, r]) for r in range(rows)]
    for copy in loads + in_x + in_og:
        copy.start()
    for copy in loads:
        copy.wait()
    depth = slab.shape[1]
    at = pl.ds(pl.multiple_of(place[3] * depth, depth), depth)
    for t in range(3):
        both[t * width : (t + 1) * width, :] = three_w[t].T
        slab[0, :, t * width : (t + 1) * width] = three_w[t, at, :]
    for r in range(rows):
        in_x[r].wait()
        three = dot_nt(both[...], rows_x[r]).astype(BF16)
        at = slice(r * HEAD_DIM, (r + 1) * HEAD_DIM)
        for t, out in enumerate((qt, kt, vt)):
            for h in range(width // HEAD_DIM):
                first = t * width + h * HEAD_DIM
                out[h, at, :] = three[first : first + HEAD_DIM]
    scores(place[0], place[1], qt, kt, turned, keep, give, 0)
    for r in range(rows):
        in_og[r].wait()
        grad = dot_nt(held_wo[...], rows_og[r]).astype(BF16)
        at = slice(r * HEAD_DIM, (r + 1) * HEAD_DIM)
        for h in range(width // HEAD_DIM):
            gt[h, at, :] = grad[h * HEAD_DIM : (h + 1) * HEAD_DIM]
    scores(place[0], place[1], gt, vt, turned, keep, give, kt.shape[2])


def pair_kernel(place, keep, got, *outs):
    for k in range(keep.shape[0]):
        outs[k][...] = (keep[k].astype(F32) + got[k].astype(F32)).astype(outs[k].dtype)


def pair_pass_kernel(place, keep, got, slab, *outs):
    pair_kernel(place, keep, got, *outs[:-1])
    outs[-1][...] = slab[...]


def join_kernel(place, *refs):
    *parts, out = refs
    at = 0
    for part in parts:
        out[at : at + part.shape[0]] = part[...]
        at += part.shape[0]


def pack_kernel(place, *refs):
    *slabs, out = refs
    at = 0
    for slab in slabs:
        count, depth, wide = slab.shape
        folds = out.shape[1] // wide
        rows = depth // folds
        for z in range(count):
            for i in range(folds):
                out[at : at + rows, i * wide : (i + 1) * wide] = slab[z, i * rows : (i + 1) * rows]
            at += rows


def added(parts, cols=slice(None)):
    total = parts[0][:, cols].astype(F32)
    for part in parts[1:]:
        total = total + part[:, cols].astype(F32)
    return total


def score_kernel(logit_scale, place, *refs):
    *parts, out = refs
    cols = out.shape[1] // 2
    exponent = jnp.exp(added(parts, slice(0, cols)) * logit_scale)
    probs = exponent / jnp.sum(exponent, axis=1, keepdims=True)
    out[:, 0:cols] = probs.astype(BF16)
    grad = added(parts, slice(cols, None))
    inner = jnp.sum(probs * grad, axis=1, keepdims=True)
    out[:, cols:] = (logit_scale * probs * (grad - inner)).astype(BF16)


def assemble(place, mine, other, full):
    piece_rows = mine[0].shape[0]
    for k in range(len(mine)):
        base = 2 * jnp.bitwise_xor(place[0], k)
        for side, part in ((place[1], mine[k]), (1 - place[1], other[k])):
            at = pl.ds(pl.multiple_of((base + side) * piece_rows, piece_rows), piece_rows)
            full[at, :] = part[0:piece_rows].astype(full.dtype)


def grads_kernel(pieces, place, *refs):
    mine, other = refs[0:pieces], refs[pieces : 2 * pieces]
    qt, kt, vt, gt = refs[2 * pieces : 2 * pieces + 4]
    send_far, four_far, full, send, four, sems = refs[2 * pieces + 4 :]
    zeds = send.shape[0]
    heads, _, cols = qt.shape
    stacked, tokens = four.shape
    rows, width, block = tokens // cols, stacked // 4, cols // zeds
    assemble(place, mine, other, full)
    copies = []
    for h in range(heads):
        span = slice(h * cols, (h + 1) * cols)
        values = (
            dot_nt(kt[h], full[span, cols:]),
            dot_nn(qt[h], full[span, cols:]),
            dot_nn(gt[h], full[span, 0:cols]),
            dot_nt(vt[h], full[span, 0:cols]),
        )
        for t, value in enumerate(values):
            value = value.astype(BF16)
            at = slice(t * width + h * HEAD_DIM, t * width + (h + 1) * HEAD_DIM)
            for r in range(rows):
                part = value[r * HEAD_DIM : (r + 1) * HEAD_DIM]
                four[at, r * cols : (r + 1) * cols] = part
                if t < 3:
                    for z in range(zeds):
                        cut = part[:, z * block : (z + 1) * block]
                        send[z, at, r * block : (r + 1) * block] = cut
            pairs = [(send.at[:, at], send_far.at[:, at])] if t < 3 else []
            copies += fetch(pairs + [(four.at[at], four_far.at[at])], sems.at[h * 4 + t])
    for copy in copies:
        copy.wait()


def weights_kernel(place, x_far, og_far, four_far, keep, give, x, og, four, total, sems):
    stacked, tokens = four.shape
    three = 3 * stacked // 4
    piece_rows = keep.shape[1]
    steps = sems.shape[0]
    spans = [slice(i * tokens // steps, (i + 1) * tokens // steps) for i in range(steps)]
    copies = []
    for i, span in enumerate(spans):
        pairs = [(four_far.at[:, span], four.at[:, span]), (x_far.at[span], x.at[span])]
        copies.append(fetch(pairs + [(og_far.at[span], og.at[span])], sems.at[i]))
    for i, span in enumerate(spans):
        for copy in copies[i]:
            copy.wait()
        for first, last, other in ((0, three, x), (three, stacked, og)):
            part = dot_nn(four[first:last, span], other[span, :])
            if i > 0:
                part = part + total[first:last, :]
            if i < steps - 1:
                total[first:last, :] = part
            else:
                value = part.astype(BF16)
                for j in range(first, last, piece_rows):
                    piece = value[j - first : j - first + piece_rows]
                    deal(place[0], place[1], j // piece_rows, keep, give, piece)


def pair_append_kernel(place, keep, got, packed, *outs):
    pieces, piece_rows, _ = keep.shape
    for k in range(pieces):
        outs[k][0:piece_rows] = (keep[k].astype(F32) + got[k].astype(F32)).astype(BF16)
        if outs[k].shape[0] > piece_rows:
            outs[k][piece_rows:] = packed[...]


def sum_relay_kernel(scale, place, packed, *refs):
    *parts, out, first, second, third, slabs = refs
    rows, extra = out.shape[0], packed.shape[0]
    total = parts[0][0:rows].astype(F32)
    for part in parts[1:]:
        total = total + part[0:rows].astype(F32)
    total = (total * scale).astype(out.dtype)
    out[...] = total
    cut = first.shape[0] - rows
    for target in (first, second, third):
        target[0:rows] = total
    first[rows:] = parts[2][rows : rows + cut]
    second[rows:] = parts[1][rows + cut : rows + 2 * cut]
    third[rows:] = packed[2 * cut :]
    slabs[0] = parts[1][rows:]
    slabs[1] = parts[2][rows:]


def unpack_kernel(pieces, place, *refs):
    mine, other = refs[0:pieces], refs[pieces : 2 * pieces]
    outs, full = refs[2 * pieces : -1], refs[-1]
    assemble(place, mine, other, full)
    width = full.shape[0] // len(outs)
    for t, out in enumerate(outs[:-1]):
        out[...] = full[t * width : (t + 1) * width, :].T
    outs[-1][...] = full[(len(outs) - 1) * width :, :]


def gather_weights_kernel(zeds, place, wq, wk, wv, own, own_other, near, near_other, *refs):
    *far, full = refs
    model, width = wq.shape
    wide = 3 * width
    extra = own.shape[0]
    folds = model // wide
    rows = extra // (zeds - 1)
    depth = rows * folds
    zed = place[2]
    for t, w in enumerate((wq, wk, wv)):
        full[:, pl.ds(pl.multiple_of((3 * zed + t) * width, width), width)] = w[...]
    cut = extra // 3 // 16 * 16
    skip = far[0].shape[0] - cut

    def part(side, k, first, count):
        if k == 0:
            return (own, own_other)[side][first : first + count]
        if k < 3:
            return (near, near_other)[side][k - 1, first : first + count]
        way = min(first // cut, 2)
        at = skip + first - way * cut
        return far[3 * side + way][at : at + count]

    unit = math.gcd(rows, cut)
    for k in range(4):
        base = 2 * jnp.bitwise_xor(place[3] // 2, k)
        for side, core in ((0, place[1]), (1, 1 - place[1])):
            for first in range(0, extra, unit):
                z, offset = 1 + first // rows, first % rows
                cols = pl.ds(pl.multiple_of(jnp.bitwise_xor(zed, z) * wide, width), wide)
                value = part(side, k, first, unit)
                for i in range(folds):
                    row = pl.multiple_of((base + core) * depth + i * rows + offset, unit)
                    full[pl.ds(row, unit), cols] = value[:, i * wide : (i + 1) * wide]


def inputs_kernel(place, sent_far, full, out, sent, total, sems):
    rows, block, _ = out.shape
    deep = sent.shape[0] // 2
    halves = (slice(0, deep), slice(deep, 2 * deep))
    copies = fetch([(sent_far.at[half], sent.at[half]) for half in halves], sems)
    copies[0].wait()
    total[...] = dot_nn(full[:, halves[0]], sent[halves[0], :])
    copies[1].wait()
    step = min(2, rows)
    for r in range(0, rows, step):
        span = slice(r * block, (r + step) * block)
        value = total[:, span] + dot_nn(full[:, halves[1]], sent[halves[1], span])
        value = value.astype(BF16).T
        for i in range(step):
            out[r + i] = value[i * block : (i + 1) * block]


def body(inputs, out_grad, w_query, w_key, w_value, w_output):
    rows, cols, model = inputs.shape
    width = w_query.shape[1]
    heads = width // HEAD_DIM
    merged = rows * HEAD_DIM
    seqs, zeds = lax.axis_size("seq"), lax.axis_size("head")
    pieces = seqs // 2
    all_rows = rows * seqs
    logit_scale = 1.0 / (math.sqrt(HEAD_DIM) * math.sqrt(all_rows))
    inv_root = 1.0 / math.sqrt(all_rows * cols)
    shard = heads * cols // seqs
    wide = 4 * width // seqs
    block = cols // zeds
    sharers = min(seqs, SHARERS)
    depth = model // sharers
    folds = model // (3 * width)
    me = lax.axis_index("seq")
    zed = lax.axis_index("head")
    place = jnp.stack([me // 2, me % 2, zed, me % sharers]).astype(jnp.int32)

    def swap(value):
        return lax.ppermute(value, "seq", [(i, i ^ 1) for i in range(seqs)])

    def across(value, k):
        return lax.ppermute(value, "seq", [(i, i ^ (2 * k)) for i in range(seqs)])

    def along(value, k):
        return lax.ppermute(value, "head", [(i, i ^ k) for i in range(zeds)])

    def shape(*dims, dtype=BF16):
        return jax.ShapeDtypeStruct(dims, dtype)

    def spread(paired):
        return [paired[0]] + [across(paired[k], k) for k in range(1, pieces)]

    def gathered(value, count):
        mine = [value] + [across(value, k) for k in range(1, count)]
        return mine, [swap(part) for part in mine]

    blocks = shape(heads, merged, cols)
    dealt = shape(pieces, shard, 2 * cols)
    rows_in = pltpu.VMEM((rows, cols, model), BF16)
    dot_flops = 2 * rows * cols * width * model
    score_flops = 2 * heads * cols * cols * merged

    qt, kt, vt, gt, keep, give, slab = call(
        front_kernel,
        (blocks,) * 4 + (dealt,) * 2 + (shape(1, depth, 3 * width),),
        (place, inputs, out_grad, w_query, w_key, w_value, w_output),
        hbm=6,
        scratch=[
            rows_in,
            rows_in,
            pltpu.VMEM((3, model, width), BF16),
            pltpu.VMEM((width, model), BF16),
            pltpu.VMEM((3 * width, model), BF16),
            pltpu.VMEM((cols, merged), BF16),
            pltpu.SemaphoreType.DMA((3, max(4, rows))),
        ],
        flops=4 * dot_flops + 2 * score_flops,
        name="front",
    )
    *paired, slab = call(
        pair_pass_kernel,
        [shape(shard, 2 * cols)] * pieces + [shape(*slab.shape)],
        (place, keep, swap(give), slab),
        name="pair_scores",
    )
    parts = spread(paired)
    groups, span = [slab], 1
    while span < zeds:
        if span > 1:
            slab = call(join_kernel, shape(span, depth, 3 * width), (place, *groups), name="join")
        groups.append(along(slab, span))
        span *= 2
    scored = call(
        partial(score_kernel, logit_scale),
        shape(shard, 2 * cols),
        (place, *parts),
        held=(slab,),
        name="score",
    )
    packed = call(
        pack_kernel, shape((zeds - 1) * depth // folds, model), (place, *groups[1:]), name="pack"
    )
    packed_other = swap(packed)
    mine, other = gathered(scored, pieces)
    send, four = call(
        partial(grads_kernel, pieces),
        (
            pltpu.HBM((zeds, 3 * width, rows * block), BF16),
            pltpu.HBM((4 * width, rows * cols), BF16),
        ),
        (place, *mine, *other, qt, kt, vt, gt),
        held=(packed_other,),
        out_specs=(hbm_spec(), hbm_spec()),
        scratch=[
            pltpu.VMEM((heads * cols, 2 * cols), BF16),
            pltpu.VMEM((zeds, 3 * width, rows * block), BF16),
            pltpu.VMEM((4 * width, rows * cols), BF16),
            pltpu.SemaphoreType.DMA((heads * 4, 2)),
        ],
        flops=4 * score_flops,
        name="grads",
    )
    sent = lax.all_to_all(send, "head", 0, 0, tiled=True)

    keep, give = call(
        weights_kernel,
        [shape(pieces, wide, model)] * 2,
        (place, inputs.reshape(-1, model), out_grad.reshape(-1, model), four),
        hbm=3,
        scratch=[
            pltpu.VMEM((rows * cols, model), BF16),
            pltpu.VMEM((rows * cols, model), BF16),
            pltpu.VMEM((4 * width, rows * cols), BF16),
            pltpu.VMEM((4 * width, model), F32),
            pltpu.SemaphoreType.DMA((rows, 3)),
        ],
        flops=4 * dot_flops,
        moved=inputs.size * 4,
        name="weights",
    )
    extra = packed.shape[0]
    cut = extra // 48 * 16
    near = (1, 2)
    paired = call(
        pair_append_kernel,
        [shape(wide + (extra if k in near else 0), model) for k in range(pieces)],
        (place, keep, swap(give), packed),
        name="pair_weights",
    )
    parts = spread(paired)
    total_w, first, second, third, slabs = call(
        partial(sum_relay_kernel, inv_root),
        (
            shape(wide, model),
            shape(wide + cut, model),
            shape(wide + cut, model),
            shape(wide + extra - 2 * cut, model),
            shape(2, extra, model),
        ),
        (place, packed, *parts),
        name="sum_weights",
    )
    sums = [total_w, first, second, third] + [total_w] * (pieces - 4)
    mine = [total_w] + [across(sums[k], k) for k in range(1, pieces)]
    other = [swap(part) for part in mine]
    full = call(
        partial(gather_weights_kernel, zeds),
        shape(model, zeds * 3 * width),
        (place, w_query, w_key, w_value, packed, packed_other, slabs, swap(slabs))
        + (*mine[1:4], *other[1:4]),
        name="gather_weights",
    )
    grad_q, grad_k, grad_v, grad_o = call(
        partial(unpack_kernel, pieces),
        [shape(model, width, dtype=F32)] * 3 + [shape(width, model, dtype=F32)],
        (place, *mine, *other),
        scratch=[pltpu.VMEM((4 * width, model), F32)],
        name="unpack",
    )
    grad_inputs = call(
        inputs_kernel,
        shape(rows, block, model),
        (place, sent.reshape(-1, rows * block), full),
        hbm=1,
        scratch=[
            pltpu.VMEM((zeds * 3 * width, rows * block), BF16),
            pltpu.VMEM((model, rows * block), F32),
            pltpu.SemaphoreType.DMA((2,)),
        ],
        flops=3 * dot_flops,
        name="inputs",
    )
    return (grad_inputs, grad_q, grad_k, grad_v, grad_o)


def solution(mesh):
    return jax.shard_map(
        body,
        mesh=mesh,
        in_specs=(
            P("seq", None, None),
            P("seq", None, None),
            P(None, "head"),
            P(None, "head"),
            P(None, "head"),
            P("head", None),
        ),
        out_specs=(
            P("seq", "head", None),
            P(None, "head"),
            P(None, "head"),
            P(None, "head"),
            P("head", None),
        ),
        check_vma=False,
    )
```

```python
import math
from functools import partial

import jax
import jax.numpy as jnp
from jax import lax
from jax.experimental import pallas as pl
from jax.experimental.pallas import tpu as pltpu
from jax.sharding import PartitionSpec as P

HEAD_DIM = 64
F32 = jnp.float32
BF16 = jnp.bfloat16
VMEM_BYTES = 16 * 1024 * 1024
SHARERS = 8


def dot_nn(left, right):
    return lax.dot_general(left, right, (((1,), (0,)), ((), ())), preferred_element_type=F32)


def dot_nt(left, right):
    return lax.dot_general(left, right, (((1,), (1,)), ((), ())), preferred_element_type=F32)


def vmem_spec():
    return pl.BlockSpec(memory_space=pltpu.VMEM)


def smem_spec():
    return pl.BlockSpec(memory_space=pltpu.SMEM)


def hbm_spec():
    return pl.BlockSpec(memory_space=pltpu.HBM)


def any_spec():
    return pl.BlockSpec(memory_space=pl.ANY)


def call(kernel, outs, ins, hbm=0, held=(), out_specs=None, scratch=(), flops=0, moved=0, name=None):
    count = len(ins)

    def run(*refs):
        kernel(*refs[:count], *refs[count + len(held) :])

    place, far, near = ins[0], ins[1 : 1 + hbm], ins[1 + hbm :]
    return pl.pallas_call(
        run,
        out_shape=outs,
        in_specs=[smem_spec()]
        + [hbm_spec()] * len(far)
        + [vmem_spec()] * len(near)
        + [any_spec()] * len(held),
        out_specs=out_specs or jax.tree.map(lambda _: vmem_spec(), outs),
        scratch_shapes=list(scratch),
        compiler_params=pltpu.CompilerParams(vmem_limit_bytes=VMEM_BYTES),
        cost_estimate=pl.CostEstimate(flops=flops, bytes_accessed=moved, transcendentals=0),
        name=name,
    )(place, *[far_array(x) for x in far], *near, *held)


def far_array(x):
    return pltpu.with_memory_space_constraint(x, pltpu.HBM)


def fetch(pairs, sems):
    copies = [pltpu.make_async_copy(src, dst, sems.at[i]) for i, (src, dst) in enumerate(pairs)]
    for copy in copies:
        copy.start()
    return copies


def deal(chip, core, shard, keep, give, value, first=0):
    rows = keep.shape[1]
    cols = slice(first, first + value.shape[1])
    mine = core == 0
    for i in range(0, value.shape[0], 2 * rows):
        even, odd = value[i : i + rows], value[i + rows : i + 2 * rows]
        slot = jnp.bitwise_xor(chip, (shard + i // rows) // 2)
        keep[slot, :, cols] = jnp.where(mine, even, odd)
        give[slot, :, cols] = jnp.where(mine, odd, even)


def scores(chip, core, left, right, turned, keep, give, first):
    heads, _, cols = left.shape
    piece_rows = keep.shape[1]
    for h in range(heads):
        turned[...] = left[h].T
        total = dot_nn(turned[...], right[h]).astype(BF16)
        deal(chip, core, h * cols // piece_rows, keep, give, total, first)


def front_kernel(
    place, x, og, wq, wk, wv, wo, qt, kt, vt, gt, keep, give, slab,
    rows_x, rows_og, three_w, held_wo, both, turned, sems,
):
    rows = x.shape[0]
    width = wq.shape[1]
    loads = [pltpu.make_async_copy(w, three_w.at[t], sems.at[2, t]) for t, w in enumerate((wq, wk, wv))]
    loads.append(pltpu.make_async_copy(wo, held_wo, sems.at[2, 3]))
    span = max(1, rows // 2)
    spans = [pl.ds(r, span) for r in range(0, rows, span)]
    in_x = [pltpu.make_async_copy(x.at[at], rows_x.at[at], sems.at[0, i]) for i, at in enumerate(spans)]
    in_og = [pltpu.make_async_copy(og, rows_og, sems.at[1, 0])]
    for copy in loads + in_x + in_og:
        copy.start()
    for copy in loads:
        copy.wait()
    depth = slab.shape[1]
    at = pl.ds(pl.multiple_of(place[3] * depth, depth), depth)
    for t in range(3):
        both[t * width : (t + 1) * width, :] = three_w[t].T
        slab[0, :, t * width : (t + 1) * width] = three_w[t, at, :]
    for r in range(rows):
        if r % span == 0:
            in_x[r // span].wait()
        three = dot_nt(both[...], rows_x[r]).astype(BF16)
        at = slice(r * HEAD_DIM, (r + 1) * HEAD_DIM)
        for t, out in enumerate((qt, kt, vt)):
            for h in range(width // HEAD_DIM):
                first = t * width + h * HEAD_DIM
                out[h, at, :] = three[first : first + HEAD_DIM]
    scores(place[0], place[1], qt, kt, turned, keep, give, 0)
    in_og[0].wait()
    for r in range(rows):
        grad = dot_nt(held_wo[...], rows_og[r]).astype(BF16)
        at = slice(r * HEAD_DIM, (r + 1) * HEAD_DIM)
        for h in range(width // HEAD_DIM):
            gt[h, at, :] = grad[h * HEAD_DIM : (h + 1) * HEAD_DIM]
    scores(place[0], place[1], gt, vt, turned, keep, give, kt.shape[2])


def pair_kernel(place, keep, got, *outs):
    for k in range(keep.shape[0]):
        outs[k][...] = (keep[k].astype(F32) + got[k].astype(F32)).astype(outs[k].dtype)


def pair_pass_kernel(place, keep, got, slab, *outs):
    pair_kernel(place, keep, got, *outs[:-1])
    outs[-1][...] = slab[...]


def join_kernel(place, *refs):
    *parts, out = refs
    at = 0
    for part in parts:
        out[at : at + part.shape[0]] = part[...]
        at += part.shape[0]


def pack_kernel(place, *refs):
    *slabs, out = refs
    at = 0
    for slab in slabs:
        count, depth, wide = slab.shape
        folds = out.shape[1] // wide
        rows = depth // folds
        for z in range(count):
            for i in range(folds):
                out[at : at + rows, i * wide : (i + 1) * wide] = slab[z, i * rows : (i + 1) * rows]
            at += rows


def added(parts, cols=slice(None)):
    total = parts[0][:, cols].astype(F32)
    for part in parts[1:]:
        total = total + part[:, cols].astype(F32)
    return total


def score_kernel(logit_scale, place, *refs):
    *parts, out = refs
    cols = out.shape[1] // 2
    exponent = jnp.exp(added(parts, slice(0, cols)) * logit_scale)
    probs = exponent / jnp.sum(exponent, axis=1, keepdims=True)
    out[:, 0:cols] = probs.astype(BF16)
    grad = added(parts, slice(cols, None))
    inner = jnp.sum(probs * grad, axis=1, keepdims=True)
    out[:, cols:] = (logit_scale * probs * (grad - inner)).astype(BF16)


def assemble(place, mine, other, full):
    piece_rows = mine[0].shape[0]
    for k in range(len(mine)):
        base = 2 * jnp.bitwise_xor(place[0], k)
        for side, part in ((place[1], mine[k]), (1 - place[1], other[k])):
            at = pl.ds(pl.multiple_of((base + side) * piece_rows, piece_rows), piece_rows)
            full[at, :] = part[0:piece_rows].astype(full.dtype)


def grads_kernel(pieces, place, *refs):
    mine, other = refs[0:pieces], refs[pieces : 2 * pieces]
    qt, kt, vt, gt = refs[2 * pieces : 2 * pieces + 4]
    send_far, four_far, full, send, four, sems = refs[2 * pieces + 4 :]
    zeds = send.shape[0]
    heads, _, cols = qt.shape
    stacked, tokens = four.shape
    rows, width, block = tokens // cols, stacked // 4, cols // zeds
    assemble(place, mine, other, full)
    copies = []
    for h in range(heads):
        span = slice(h * cols, (h + 1) * cols)
        values = (
            dot_nt(kt[h], full[span, cols:]),
            dot_nn(qt[h], full[span, cols:]),
            dot_nn(gt[h], full[span, 0:cols]),
            dot_nt(vt[h], full[span, 0:cols]),
        )
        for t, value in enumerate(values):
            value = value.astype(BF16)
            at = slice(t * width + h * HEAD_DIM, t * width + (h + 1) * HEAD_DIM)
            for r in range(rows):
                part = value[r * HEAD_DIM : (r + 1) * HEAD_DIM]
                four[at, r * cols : (r + 1) * cols] = part
                if t < 3:
                    for z in range(zeds):
                        cut = part[:, z * block : (z + 1) * block]
                        send[z, at, r * block : (r + 1) * block] = cut
            pairs = [(send.at[:, at], send_far.at[:, at])] if t < 3 else []
            copies += fetch(pairs + [(four.at[at], four_far.at[at])], sems.at[h * 4 + t])
    for copy in copies:
        copy.wait()


def weights_kernel(place, x_far, og_far, four_far, keep, give, x, og, four, total, sems):
    stacked, tokens = four.shape
    three = 3 * stacked // 4
    piece_rows = keep.shape[1]
    steps = sems.shape[0]
    spans = [slice(i * tokens // steps, (i + 1) * tokens // steps) for i in range(steps)]
    copies = []
    for i, span in enumerate(spans):
        pairs = [(four_far.at[:, span], four.at[:, span]), (x_far.at[span], x.at[span])]
        copies.append(fetch(pairs + [(og_far.at[span], og.at[span])], sems.at[i]))
    for i, span in enumerate(spans):
        for copy in copies[i]:
            copy.wait()
        for first, last, other in ((0, three, x), (three, stacked, og)):
            part = dot_nn(four[first:last, span], other[span, :])
            if i > 0:
                part = part + total[first:last, :]
            if i < steps - 1:
                total[first:last, :] = part
            else:
                deal(place[0], place[1], first // piece_rows, keep, give, part.astype(BF16))


def pair_append_kernel(place, keep, got, packed, *outs):
    pieces, piece_rows, _ = keep.shape
    for k in range(pieces):
        outs[k][0:piece_rows] = (keep[k].astype(F32) + got[k].astype(F32)).astype(BF16)
        if outs[k].shape[0] > piece_rows:
            outs[k][piece_rows:] = packed[...]


def sum_relay_kernel(scale, place, packed, *refs):
    *parts, out, first, second, third, slabs = refs
    rows, extra = out.shape[0], packed.shape[0]
    total = parts[0][0:rows].astype(F32)
    for part in parts[1:]:
        total = total + part[0:rows].astype(F32)
    total = (total * scale).astype(out.dtype)
    out[...] = total
    cut = first.shape[0] - rows
    for target in (first, second, third):
        target[0:rows] = total
    first[rows:] = parts[2][rows : rows + cut]
    second[rows:] = parts[1][rows + cut : rows + 2 * cut]
    third[rows:] = packed[2 * cut :]
    slabs[0] = parts[1][rows:]
    slabs[1] = parts[2][rows:]


def unpack_kernel(pieces, place, *refs):
    mine, other = refs[0:pieces], refs[pieces : 2 * pieces]
    outs, full = refs[2 * pieces : -1], refs[-1]
    assemble(place, mine, other, full)
    width = full.shape[0] // len(outs)
    for t, out in enumerate(outs[:-1]):
        out[...] = full[t * width : (t + 1) * width, :].T
    outs[-1][...] = full[(len(outs) - 1) * width :, :]


def gather_weights_kernel(zeds, place, own, own_other, near, near_other, *refs):
    *far, full = refs
    model = full.shape[0]
    wide = full.shape[1] // (zeds - 1)
    extra = own.shape[0]
    folds = model // wide
    rows = extra // (zeds - 1)
    depth = rows * folds
    cut = extra // 3 // 16 * 16
    skip = far[0].shape[0] - cut

    def part(side, k, first, count):
        if k == 0:
            return (own, own_other)[side][first : first + count]
        if k < 3:
            return (near, near_other)[side][k - 1, first : first + count]
        way = min(first // cut, 2)
        at = skip + first - way * cut
        return far[3 * side + way][at : at + count]

    unit = math.gcd(rows, cut)
    for k in range(4):
        base = 2 * jnp.bitwise_xor(place[3] // 2, k)
        for side, core in ((0, place[1]), (1, 1 - place[1])):
            for first in range(0, extra, unit):
                z, offset = 1 + first // rows, first % rows
                cols = slice((z - 1) * wide, z * wide)
                value = part(side, k, first, unit)
                for i in range(folds):
                    row = pl.multiple_of((base + core) * depth + i * rows + offset, unit)
                    full[pl.ds(row, unit), cols] = value[:, i * wide : (i + 1) * wide]


def own_inputs_kernel(place, send_far, wq, wk, wv, total, send, full, sems):
    width = wq.shape[1]
    pairs = [(w, full.at[:, t * width : (t + 1) * width]) for t, w in enumerate((wq, wk, wv))]
    for copy in fetch([(send_far.at[place[2]], send)] + pairs, sems):
        copy.wait()
    total[...] = dot_nn(full[...], send[...])


def inputs_kernel(place, sent_far, own_part, full, out, sent, sems):
    rows, block, _ = out.shape
    zeds, depth, _ = sent_far.shape
    pairs = []
    for k in range(1, zeds):
        far = sent_far.at[jnp.bitwise_xor(place[2], k)]
        pairs.append((far, sent.at[(k - 1) * depth : k * depth]))
    for copy in fetch(pairs, sems):
        copy.wait()
    step = min(2, rows)
    for r in range(0, rows, step):
        span = slice(r * block, (r + step) * block)
        value = own_part[:, span] + dot_nn(full[...], sent[:, span])
        value = value.astype(BF16).T
        for i in range(step):
            out[r + i] = value[i * block : (i + 1) * block]


def body(inputs, out_grad, w_query, w_key, w_value, w_output):
    rows, cols, model = inputs.shape
    width = w_query.shape[1]
    heads = width // HEAD_DIM
    merged = rows * HEAD_DIM
    seqs, zeds = lax.axis_size("seq"), lax.axis_size("head")
    pieces = seqs // 2
    all_rows = rows * seqs
    logit_scale = 1.0 / (math.sqrt(HEAD_DIM) * math.sqrt(all_rows))
    inv_root = 1.0 / math.sqrt(all_rows * cols)
    shard = heads * cols // seqs
    wide = 4 * width // seqs
    block = cols // zeds
    sharers = min(seqs, SHARERS)
    depth = model // sharers
    folds = model // (3 * width)
    me = lax.axis_index("seq")
    zed = lax.axis_index("head")
    place = jnp.stack([me // 2, me % 2, zed, me % sharers]).astype(jnp.int32)

    def swap(value):
        return lax.ppermute(value, "seq", [(i, i ^ 1) for i in range(seqs)])

    def across(value, k):
        return lax.ppermute(value, "seq", [(i, i ^ (2 * k)) for i in range(seqs)])

    def along(value, k):
        return lax.ppermute(value, "head", [(i, i ^ k) for i in range(zeds)])

    def shape(*dims, dtype=BF16):
        return jax.ShapeDtypeStruct(dims, dtype)

    def spread(paired):
        return [paired[0]] + [across(paired[k], k) for k in range(1, pieces)]

    def gathered(value, count):
        mine = [value] + [across(value, k) for k in range(1, count)]
        return mine, [swap(part) for part in mine]

    blocks = shape(heads, merged, cols)
    dealt = shape(pieces, shard, 2 * cols)
    rows_in = pltpu.VMEM((rows, cols, model), BF16)
    dot_flops = 2 * rows * cols * width * model
    score_flops = 2 * heads * cols * cols * merged

    qt, kt, vt, gt, keep, give, slab = call(
        front_kernel,
        (blocks,) * 4 + (dealt,) * 2 + (shape(1, depth, 3 * width),),
        (place, inputs, out_grad, w_query, w_key, w_value, w_output),
        hbm=6,
        scratch=[
            rows_in,
            rows_in,
            pltpu.VMEM((3, model, width), BF16),
            pltpu.VMEM((width, model), BF16),
            pltpu.VMEM((3 * width, model), BF16),
            pltpu.VMEM((cols, merged), BF16),
            pltpu.SemaphoreType.DMA((3, max(4, rows))),
        ],
        flops=4 * dot_flops + 2 * score_flops,
        name="front",
    )
    *paired, slab = call(
        pair_pass_kernel,
        [shape(shard, 2 * cols)] * pieces + [shape(*slab.shape)],
        (place, keep, swap(give), slab),
        name="pair_scores",
    )
    parts = spread(paired)
    groups, span = [slab], 1
    while span < zeds:
        if span > 1:
            slab = call(join_kernel, shape(span, depth, 3 * width), (place, *groups), name="join")
        groups.append(along(slab, span))
        span *= 2
    scored = call(
        partial(score_kernel, logit_scale),
        shape(shard, 2 * cols),
        (place, *parts),
        held=(slab,),
        name="score",
    )
    swapped = [swap(group) for group in groups[1:]]
    mine, other = gathered(scored, pieces)
    send, four = call(
        partial(grads_kernel, pieces),
        (
            pltpu.HBM((zeds, 3 * width, rows * block), BF16),
            pltpu.HBM((4 * width, rows * cols), BF16),
        ),
        (place, *mine, *other, qt, kt, vt, gt),
        held=swapped[1:] or swapped,
        out_specs=(hbm_spec(), hbm_spec()),
        scratch=[
            pltpu.VMEM((heads * cols, 2 * cols), BF16),
            pltpu.VMEM((zeds, 3 * width, rows * block), BF16),
            pltpu.VMEM((4 * width, rows * cols), BF16),
            pltpu.SemaphoreType.DMA((heads * 4, 2)),
        ],
        flops=4 * score_flops,
        name="grads",
    )
    own_part = call(
        own_inputs_kernel,
        shape(model, rows * block, dtype=F32),
        (place, send, w_query, w_key, w_value),
        hbm=4,
        scratch=[
            pltpu.VMEM((3 * width, rows * block), BF16),
            pltpu.VMEM((model, 3 * width), BF16),
            pltpu.SemaphoreType.DMA((4,)),
        ],
        flops=3 * dot_flops // zeds,
        name="own_inputs",
    )
    sent = lax.all_to_all(send, "head", 0, 0, tiled=True)

    keep, give = call(
        weights_kernel,
        [shape(pieces, wide, model)] * 2,
        (place, inputs.reshape(-1, model), out_grad.reshape(-1, model), four),
        hbm=3,
        scratch=[
            pltpu.VMEM((rows * cols, model), BF16),
            pltpu.VMEM((rows * cols, model), BF16),
            pltpu.VMEM((4 * width, rows * cols), BF16),
            pltpu.VMEM((4 * width, model), F32),
            pltpu.SemaphoreType.DMA((rows, 3)),
        ],
        flops=4 * dot_flops,
        moved=inputs.size * 4,
        name="weights",
    )
    packed, packed_other = [
        call(pack_kernel, shape((zeds - 1) * depth // folds, model), (place, *parts), name="pack")
        for parts in (groups[1:], swapped)
    ]
    extra = packed.shape[0]
    cut = extra // 48 * 16
    near = (1, 2)
    paired = call(
        pair_append_kernel,
        [shape(wide + (extra if k in near else 0), model) for k in range(pieces)],
        (place, keep, swap(give), packed),
        name="pair_weights",
    )
    parts = spread(paired)
    total_w, first, second, third, slabs = call(
        partial(sum_relay_kernel, inv_root),
        (
            shape(wide, model),
            shape(wide + cut, model),
            shape(wide + cut, model),
            shape(wide + extra - 2 * cut, model),
            shape(2, extra, model),
        ),
        (place, packed, *parts),
        held=(own_part,),
        name="sum_weights",
    )
    sums = [total_w, first, second, third] + [total_w] * (pieces - 4)
    mine = [total_w] + [across(sums[k], k) for k in range(1, pieces)]
    other = [swap(part) for part in mine]
    full = call(
        partial(gather_weights_kernel, zeds),
        shape(model, (zeds - 1) * 3 * width),
        (place, packed, packed_other, slabs, swap(slabs))
        + (*mine[1:4], *other[1:4]),
        name="gather_weights",
    )
    grad_q, grad_k, grad_v, grad_o = call(
        partial(unpack_kernel, pieces),
        [shape(model, width, dtype=F32)] * 3 + [shape(width, model, dtype=F32)],
        (place, *mine, *other),
        scratch=[pltpu.VMEM((4 * width, model), F32)],
        name="unpack",
    )
    grad_inputs = call(
        inputs_kernel,
        shape(rows, block, model),
        (place, sent, own_part, full),
        hbm=1,
        scratch=[
            pltpu.VMEM(((zeds - 1) * 3 * width, rows * block), BF16),
            pltpu.SemaphoreType.DMA((zeds - 1,)),
        ],
        flops=3 * dot_flops * (zeds - 1) // zeds,
        name="inputs",
    )
    return (grad_inputs, grad_q, grad_k, grad_v, grad_o)


def solution(mesh):
    return jax.shard_map(
        body,
        mesh=mesh,
        in_specs=(
            P("seq", None, None),
            P("seq", None, None),
            P(None, "head"),
            P(None, "head"),
            P(None, "head"),
            P("head", None),
        ),
        out_specs=(
            P("seq", "head", None),
            P(None, "head"),
            P(None, "head"),
            P(None, "head"),
            P("head", None),
        ),
        check_vma=False,
    )
```

```python
import math
from functools import partial

import jax
import jax.numpy as jnp
from jax import lax
from jax.experimental import pallas as pl
from jax.experimental.pallas import tpu as pltpu
from jax.sharding import PartitionSpec as P

HEAD_DIM = 64
F32 = jnp.float32
BF16 = jnp.bfloat16
VMEM_BYTES = 16 * 1024 * 1024
SHARERS = 8


def dot_nn(left, right):
    return lax.dot_general(left, right, (((1,), (0,)), ((), ())), preferred_element_type=F32)


def dot_nt(left, right):
    return lax.dot_general(left, right, (((1,), (1,)), ((), ())), preferred_element_type=F32)


def vmem_spec():
    return pl.BlockSpec(memory_space=pltpu.VMEM)


def smem_spec():
    return pl.BlockSpec(memory_space=pltpu.SMEM)


def hbm_spec():
    return pl.BlockSpec(memory_space=pltpu.HBM)


def any_spec():
    return pl.BlockSpec(memory_space=pl.ANY)


def call(kernel, outs, ins, hbm=0, held=(), out_specs=None, scratch=(), flops=0, moved=0, name=None):
    count = len(ins)

    def run(*refs):
        kernel(*refs[:count], *refs[count + len(held) :])

    place, far, near = ins[0], ins[1 : 1 + hbm], ins[1 + hbm :]
    return pl.pallas_call(
        run,
        out_shape=outs,
        in_specs=[smem_spec()]
        + [hbm_spec()] * len(far)
        + [vmem_spec()] * len(near)
        + [any_spec()] * len(held),
        out_specs=out_specs or jax.tree.map(lambda _: vmem_spec(), outs),
        scratch_shapes=list(scratch),
        compiler_params=pltpu.CompilerParams(vmem_limit_bytes=VMEM_BYTES),
        cost_estimate=pl.CostEstimate(flops=flops, bytes_accessed=moved, transcendentals=0),
        name=name,
    )(place, *[far_array(x) for x in far], *near, *held)


def far_array(x):
    return pltpu.with_memory_space_constraint(x, pltpu.HBM)


def fetch(pairs, sems):
    copies = [pltpu.make_async_copy(src, dst, sems.at[i]) for i, (src, dst) in enumerate(pairs)]
    for copy in copies:
        copy.start()
    return copies


def deal(chip, core, shard, keep, give, value, first=0):
    rows = keep.shape[1]
    cols = slice(first, first + value.shape[1])
    mine = core == 0
    for i in range(0, value.shape[0], 2 * rows):
        even, odd = value[i : i + rows], value[i + rows : i + 2 * rows]
        slot = jnp.bitwise_xor(chip, (shard + i // rows) // 2)
        keep[slot, :, cols] = jnp.where(mine, even, odd)
        give[slot, :, cols] = jnp.where(mine, odd, even)


def scores(chip, core, left, right, turned, keep, give, first):
    heads, _, cols = left.shape
    piece_rows = keep.shape[1]
    for h in range(heads):
        turned[...] = left[h].T
        total = dot_nn(turned[...], right[h]).astype(BF16)
        deal(chip, core, h * cols // piece_rows, keep, give, total, first)


def front_kernel(
    place, x, og, wq, wk, wv, wo, qt, kt, vt, gt, keep, give, slab,
    rows_x, rows_og, three_w, held_wo, both, turned, sems,
):
    rows = x.shape[0]
    width = wq.shape[1]
    loads = [pltpu.make_async_copy(w, three_w.at[t], sems.at[2, t]) for t, w in enumerate((wq, wk, wv))]
    loads.append(pltpu.make_async_copy(wo, held_wo, sems.at[2, 3]))
    span = max(1, rows // 2)
    spans = [pl.ds(r, span) for r in range(0, rows, span)]
    in_x = [pltpu.make_async_copy(x.at[at], rows_x.at[at], sems.at[0, i]) for i, at in enumerate(spans)]
    in_og = [pltpu.make_async_copy(og, rows_og, sems.at[1, 0])]
    for copy in loads + in_x + in_og:
        copy.start()
    for copy in loads:
        copy.wait()
    depth = slab.shape[1]
    at = pl.ds(pl.multiple_of(place[3] * depth, depth), depth)
    for t in range(3):
        both[t * width : (t + 1) * width, :] = three_w[t].T
        slab[0, :, t * width : (t + 1) * width] = three_w[t, at, :]
    for r in range(rows):
        if r % span == 0:
            in_x[r // span].wait()
        three = dot_nt(both[...], rows_x[r]).astype(BF16)
        at = slice(r * HEAD_DIM, (r + 1) * HEAD_DIM)
        for t, out in enumerate((qt, kt, vt)):
            for h in range(width // HEAD_DIM):
                first = t * width + h * HEAD_DIM
                out[h, at, :] = three[first : first + HEAD_DIM]
    scores(place[0], place[1], qt, kt, turned, keep, give, 0)
    in_og[0].wait()
    for r in range(rows):
        grad = dot_nt(held_wo[...], rows_og[r]).astype(BF16)
        at = slice(r * HEAD_DIM, (r + 1) * HEAD_DIM)
        for h in range(width // HEAD_DIM):
            gt[h, at, :] = grad[h * HEAD_DIM : (h + 1) * HEAD_DIM]
    scores(place[0], place[1], gt, vt, turned, keep, give, kt.shape[2])


def pair_kernel(place, keep, got, *outs):
    for k in range(keep.shape[0]):
        outs[k][...] = (keep[k].astype(F32) + got[k].astype(F32)).astype(outs[k].dtype)


def pair_pass_kernel(place, keep, got, slab, *outs):
    pair_kernel(place, keep, got, *outs[:-1])
    outs[-1][...] = slab[...]


def join_kernel(place, *refs):
    *parts, out = refs
    at = 0
    for part in parts:
        out[at : at + part.shape[0]] = part[...]
        at += part.shape[0]


def pack_kernel(place, *refs):
    *slabs, out = refs
    at = 0
    for slab in slabs:
        count, depth, wide = slab.shape
        folds = out.shape[1] // wide
        rows = depth // folds
        for z in range(count):
            for i in range(folds):
                out[at : at + rows, i * wide : (i + 1) * wide] = slab[z, i * rows : (i + 1) * rows]
            at += rows


def added(parts, cols=slice(None)):
    total = parts[0][:, cols].astype(F32)
    for part in parts[1:]:
        total = total + part[:, cols].astype(F32)
    return total


def score_kernel(logit_scale, place, *refs):
    *parts, out = refs
    cols = out.shape[1] // 2
    exponent = jnp.exp(added(parts, slice(0, cols)) * logit_scale)
    probs = exponent / jnp.sum(exponent, axis=1, keepdims=True)
    out[:, 0:cols] = probs.astype(BF16)
    grad = added(parts, slice(cols, None))
    inner = jnp.sum(probs * grad, axis=1, keepdims=True)
    out[:, cols:] = (logit_scale * probs * (grad - inner)).astype(BF16)


def assemble(place, mine, other, full):
    piece_rows = mine[0].shape[0]
    for k in range(len(mine)):
        base = 2 * jnp.bitwise_xor(place[0], k)
        for side, part in ((place[1], mine[k]), (1 - place[1], other[k])):
            at = pl.ds(pl.multiple_of((base + side) * piece_rows, piece_rows), piece_rows)
            full[at, :] = part[0:piece_rows].astype(full.dtype)


def grads_kernel(pieces, place, *refs):
    mine, other = refs[0:pieces], refs[pieces : 2 * pieces]
    qt, kt, vt, gt = refs[2 * pieces : 2 * pieces + 4]
    send_far, att_far, full, send, att, sems = refs[2 * pieces + 4 :]
    heads, _, cols = qt.shape
    zeds, width, tokens = att.shape
    block = cols // zeds
    assemble(place, mine, other, full)
    copies = []
    for h in range(heads):
        span = slice(h * cols, (h + 1) * cols)
        values = (
            dot_nt(kt[h], full[span, cols:]),
            dot_nn(qt[h], full[span, cols:]),
            dot_nn(gt[h], full[span, 0:cols]),
            dot_nt(vt[h], full[span, 0:cols]),
        )
        for t, value in enumerate(values):
            value = value.astype(BF16)
            near, far, at = (send, send_far, t * width) if t < 3 else (att, att_far, 0)
            at = slice(at + h * HEAD_DIM, at + (h + 1) * HEAD_DIM)
            for r in range(tokens // block):
                part = value[r * HEAD_DIM : (r + 1) * HEAD_DIM]
                for z in range(zeds):
                    near[z, at, r * block : (r + 1) * block] = part[:, z * block : (z + 1) * block]
            copies += fetch([(near.at[:, at], far.at[:, at])], sems.at[pl.ds(h * 4 + t, 1)])
    for copy in copies:
        copy.wait()


def weights_kernel(place, x_far, og_far, send_far, att_far, keep, give, x, og, send, att, total, sems):
    zeds, three, tokens = send.shape
    rows, cols, model = x_far.shape
    block = cols // zeds
    stacked = total.shape[0]
    piece_rows = keep.shape[1]
    copies = []
    for z in range(zeds):
        at = pl.ds(z * block, block)
        pairs = [(send_far.at[z], send.at[z]), (x_far.at[:, at], x.at[z])]
        copies.append(fetch(pairs + [(att_far.at[z], att.at[z]), (og_far.at[:, at], og.at[z])], sems.at[z]))
    for z in range(zeds):
        for first, last, left, right, half in ((0, three, send, x, 0), (three, stacked, att, og, 2)):
            for copy in copies[z][half : half + 2]:
                copy.wait()
            part = dot_nn(left[z], right[z].reshape(tokens, model))
            if z > 0:
                part = part + total[first:last, :]
            if z < zeds - 1:
                total[first:last, :] = part
            else:
                deal(place[0], place[1], first // piece_rows, keep, give, part.astype(BF16))


def pair_append_kernel(place, keep, got, packed, *outs):
    pieces, piece_rows, _ = keep.shape
    for k in range(pieces):
        outs[k][0:piece_rows] = (keep[k].astype(F32) + got[k].astype(F32)).astype(BF16)
        if outs[k].shape[0] > piece_rows:
            outs[k][piece_rows:] = packed[...]


def sum_relay_kernel(scale, place, packed, *refs):
    *parts, out, first, second, third, slabs = refs
    rows, extra = out.shape[0], packed.shape[0]
    total = parts[0][0:rows].astype(F32)
    for part in parts[1:]:
        total = total + part[0:rows].astype(F32)
    total = (total * scale).astype(out.dtype)
    out[...] = total
    cut = first.shape[0] - rows
    for target in (first, second, third):
        target[0:rows] = total
    first[rows:] = parts[2][rows : rows + cut]
    second[rows:] = parts[1][rows + cut : rows + 2 * cut]
    third[rows:] = packed[2 * cut :]
    slabs[0] = parts[1][rows:]
    slabs[1] = parts[2][rows:]


def unpack_kernel(pieces, place, *refs):
    mine, other = refs[0:pieces], refs[pieces : 2 * pieces]
    outs, full = refs[2 * pieces : -1], refs[-1]
    assemble(place, mine, other, full)
    width = full.shape[0] // len(outs)
    for t, out in enumerate(outs[:-1]):
        out[...] = full[t * width : (t + 1) * width, :].T
    outs[-1][...] = full[(len(outs) - 1) * width :, :]


def gather_weights_kernel(zeds, place, own, own_other, near, near_other, *refs):
    *far, full = refs
    model = full.shape[0]
    wide = full.shape[1] // (zeds - 1)
    extra = own.shape[0]
    folds = model // wide
    rows = extra // (zeds - 1)
    depth = rows * folds
    cut = extra // 3 // 16 * 16
    skip = far[0].shape[0] - cut

    def part(side, k, first, count):
        if k == 0:
            return (own, own_other)[side][first : first + count]
        if k < 3:
            return (near, near_other)[side][k - 1, first : first + count]
        way = min(first // cut, 2)
        at = skip + first - way * cut
        return far[3 * side + way][at : at + count]

    unit = math.gcd(rows, cut)
    for k in range(4):
        base = 2 * jnp.bitwise_xor(place[3] // 2, k)
        for side, core in ((0, place[1]), (1, 1 - place[1])):
            for first in range(0, extra, unit):
                z, offset = 1 + first // rows, first % rows
                cols = slice((z - 1) * wide, z * wide)
                value = part(side, k, first, unit)
                for i in range(folds):
                    row = pl.multiple_of((base + core) * depth + i * rows + offset, unit)
                    full[pl.ds(row, unit), cols] = value[:, i * wide : (i + 1) * wide]


def own_inputs_kernel(place, send_far, wq, wk, wv, total, send, full, sems):
    width = wq.shape[1]
    pairs = [(w, full.at[:, t * width : (t + 1) * width]) for t, w in enumerate((wq, wk, wv))]
    for copy in fetch([(send_far.at[place[2]], send)] + pairs, sems):
        copy.wait()
    total[...] = dot_nn(full[...], send[...])


def inputs_kernel(place, sent_far, own_part, full, out_far, sent, out, sems):
    rows, block, _ = out.shape
    zeds, depth, _ = sent_far.shape
    pairs = []
    for k in range(1, zeds):
        far = sent_far.at[jnp.bitwise_xor(place[2], k)]
        pairs.append((far, sent.at[(k - 1) * depth : k * depth]))
    for copy in fetch(pairs, sems.at[0]):
        copy.wait()
    step = min(2, rows)
    copies = []
    for r in range(0, rows, step):
        span = slice(r * block, (r + step) * block)
        value = own_part[:, span] + dot_nn(full[...], sent[:, span])
        value = value.astype(BF16).T
        for i in range(step):
            out[r + i] = value[i * block : (i + 1) * block]
        here = pl.ds(r, step)
        copies += fetch([(out.at[here], out_far.at[here])], sems.at[1, pl.ds(r // step, 1)])
    for copy in copies:
        copy.wait()


def body(inputs, out_grad, w_query, w_key, w_value, w_output):
    rows, cols, model = inputs.shape
    width = w_query.shape[1]
    heads = width // HEAD_DIM
    merged = rows * HEAD_DIM
    seqs, zeds = lax.axis_size("seq"), lax.axis_size("head")
    pieces = seqs // 2
    all_rows = rows * seqs
    logit_scale = 1.0 / (math.sqrt(HEAD_DIM) * math.sqrt(all_rows))
    inv_root = 1.0 / math.sqrt(all_rows * cols)
    shard = heads * cols // seqs
    wide = 4 * width // seqs
    block = cols // zeds
    sharers = min(seqs, SHARERS)
    depth = model // sharers
    folds = model // (3 * width)
    me = lax.axis_index("seq")
    zed = lax.axis_index("head")
    place = jnp.stack([me // 2, me % 2, zed, me % sharers]).astype(jnp.int32)

    def swap(value):
        return lax.ppermute(value, "seq", [(i, i ^ 1) for i in range(seqs)])

    def across(value, k):
        return lax.ppermute(value, "seq", [(i, i ^ (2 * k)) for i in range(seqs)])

    def along(value, k):
        return lax.ppermute(value, "head", [(i, i ^ k) for i in range(zeds)])

    def shape(*dims, dtype=BF16):
        return jax.ShapeDtypeStruct(dims, dtype)

    def spread(paired):
        return [paired[0]] + [across(paired[k], k) for k in range(1, pieces)]

    def gathered(value, count):
        mine = [value] + [across(value, k) for k in range(1, count)]
        return mine, [swap(part) for part in mine]

    blocks = shape(heads, merged, cols)
    dealt = shape(pieces, shard, 2 * cols)
    rows_in = pltpu.VMEM((rows, cols, model), BF16)
    dot_flops = 2 * rows * cols * width * model
    score_flops = 2 * heads * cols * cols * merged

    qt, kt, vt, gt, keep, give, slab = call(
        front_kernel,
        (blocks,) * 4 + (dealt,) * 2 + (shape(1, depth, 3 * width),),
        (place, inputs, out_grad, w_query, w_key, w_value, w_output),
        hbm=6,
        scratch=[
            rows_in,
            rows_in,
            pltpu.VMEM((3, model, width), BF16),
            pltpu.VMEM((width, model), BF16),
            pltpu.VMEM((3 * width, model), BF16),
            pltpu.VMEM((cols, merged), BF16),
            pltpu.SemaphoreType.DMA((3, max(4, rows))),
        ],
        flops=4 * dot_flops + 2 * score_flops,
        name="front",
    )
    *paired, slab = call(
        pair_pass_kernel,
        [shape(shard, 2 * cols)] * pieces + [shape(*slab.shape)],
        (place, keep, swap(give), slab),
        name="pair_scores",
    )
    parts = spread(paired)
    groups, span = [slab], 1
    while span < zeds:
        if span > 1:
            slab = call(join_kernel, shape(span, depth, 3 * width), (place, *groups), name="join")
        groups.append(along(slab, span))
        span *= 2
    scored = call(
        partial(score_kernel, logit_scale),
        shape(shard, 2 * cols),
        (place, *parts),
        held=(slab,),
        name="score",
    )
    swapped = [swap(group) for group in groups[1:]]
    mine, other = gathered(scored, pieces)
    send, att = call(
        partial(grads_kernel, pieces),
        (
            pltpu.HBM((zeds, 3 * width, rows * block), BF16),
            pltpu.HBM((zeds, width, rows * block), BF16),
        ),
        (place, *mine, *other, qt, kt, vt, gt),
        held=swapped[1:] or swapped,
        out_specs=(hbm_spec(), hbm_spec()),
        scratch=[
            pltpu.VMEM((heads * cols, 2 * cols), BF16),
            pltpu.VMEM((zeds, 3 * width, rows * block), BF16),
            pltpu.VMEM((zeds, width, rows * block), BF16),
            pltpu.SemaphoreType.DMA((heads * 4,)),
        ],
        flops=4 * score_flops,
        name="grads",
    )
    own_part = call(
        own_inputs_kernel,
        shape(model, rows * block, dtype=F32),
        (place, send, w_query, w_key, w_value),
        hbm=4,
        scratch=[
            pltpu.VMEM((3 * width, rows * block), BF16),
            pltpu.VMEM((model, 3 * width), BF16),
            pltpu.SemaphoreType.DMA((4,)),
        ],
        flops=3 * dot_flops // zeds,
        name="own_inputs",
    )
    sent = lax.all_to_all(send, "head", 0, 0, tiled=True)

    keep, give = call(
        weights_kernel,
        [shape(pieces, wide, model)] * 2,
        (place, inputs, out_grad, send, att),
        hbm=4,
        scratch=[
            pltpu.VMEM((zeds, rows, block, model), BF16),
            pltpu.VMEM((zeds, rows, block, model), BF16),
            pltpu.VMEM((zeds, 3 * width, rows * block), BF16),
            pltpu.VMEM((zeds, width, rows * block), BF16),
            pltpu.VMEM((4 * width, model), F32),
            pltpu.SemaphoreType.DMA((zeds, 4)),
        ],
        flops=4 * dot_flops,
        moved=inputs.size * 4,
        name="weights",
    )
    packed, packed_other = [
        call(pack_kernel, shape((zeds - 1) * depth // folds, model), (place, *parts), name="pack")
        for parts in (groups[1:], swapped)
    ]
    extra = packed.shape[0]
    cut = extra // 48 * 16
    near = (1, 2)
    paired = call(
        pair_append_kernel,
        [shape(wide + (extra if k in near else 0), model) for k in range(pieces)],
        (place, keep, swap(give), packed),
        name="pair_weights",
    )
    parts = spread(paired)
    total_w, first, second, third, slabs = call(
        partial(sum_relay_kernel, inv_root),
        (
            shape(wide, model),
            shape(wide + cut, model),
            shape(wide + cut, model),
            shape(wide + extra - 2 * cut, model),
            shape(2, extra, model),
        ),
        (place, packed, *parts),
        held=(own_part,),
        name="sum_weights",
    )
    sums = [total_w, first, second, third] + [total_w] * (pieces - 4)
    mine = [total_w] + [across(sums[k], k) for k in range(1, pieces)]
    other = [swap(part) for part in mine]
    full = call(
        partial(gather_weights_kernel, zeds),
        shape(model, (zeds - 1) * 3 * width),
        (place, packed, packed_other, slabs, swap(slabs))
        + (*mine[1:4], *other[1:4]),
        name="gather_weights",
    )
    grad_q, grad_k, grad_v, grad_o = call(
        partial(unpack_kernel, pieces),
        [shape(model, width, dtype=F32)] * 3 + [shape(width, model, dtype=F32)],
        (place, *mine, *other),
        scratch=[pltpu.VMEM((4 * width, model), F32)],
        name="unpack",
    )
    grad_inputs = call(
        inputs_kernel,
        pltpu.HBM((rows, block, model), BF16),
        (place, sent, own_part, full),
        hbm=1,
        scratch=[
            pltpu.VMEM(((zeds - 1) * 3 * width, rows * block), BF16),
            pltpu.VMEM((rows, block, model), BF16),
            pltpu.SemaphoreType.DMA((2, max(zeds, rows))),
        ],
        out_specs=hbm_spec(),
        flops=3 * dot_flops * (zeds - 1) // zeds,
        name="inputs",
    )
    return (grad_inputs, grad_q, grad_k, grad_v, grad_o)


def solution(mesh):
    return jax.shard_map(
        body,
        mesh=mesh,
        in_specs=(
            P("seq", None, None),
            P("seq", None, None),
            P(None, "head"),
            P(None, "head"),
            P(None, "head"),
            P("head", None),
        ),
        out_specs=(
            P("seq", "head", None),
            P(None, "head"),
            P(None, "head"),
            P(None, "head"),
            P("head", None),
        ),
        check_vma=False,
    )
```

```python
import math
from functools import partial

import jax
import jax.numpy as jnp
from jax import lax
from jax.experimental import pallas as pl
from jax.experimental.pallas import tpu as pltpu
from jax.sharding import PartitionSpec as P

HEAD_DIM = 64
F32 = jnp.float32
BF16 = jnp.bfloat16
VMEM_BYTES = 16 * 1024 * 1024
SHARERS = 8


def dot_nn(left, right):
    return lax.dot_general(left, right, (((1,), (0,)), ((), ())), preferred_element_type=F32)


def dot_nt(left, right):
    return lax.dot_general(left, right, (((1,), (1,)), ((), ())), preferred_element_type=F32)


def vmem_spec():
    return pl.BlockSpec(memory_space=pltpu.VMEM)


def smem_spec():
    return pl.BlockSpec(memory_space=pltpu.SMEM)


def hbm_spec():
    return pl.BlockSpec(memory_space=pltpu.HBM)


def any_spec():
    return pl.BlockSpec(memory_space=pl.ANY)


def call(kernel, outs, ins, hbm=0, held=(), out_specs=None, scratch=(), flops=0, moved=0, name=None):
    count = len(ins)

    def run(*refs):
        kernel(*refs[:count], *refs[count + len(held) :])

    place, far, near = ins[0], ins[1 : 1 + hbm], ins[1 + hbm :]
    return pl.pallas_call(
        run,
        out_shape=outs,
        in_specs=[smem_spec()]
        + [hbm_spec()] * len(far)
        + [vmem_spec()] * len(near)
        + [any_spec()] * len(held),
        out_specs=out_specs or jax.tree.map(lambda _: vmem_spec(), outs),
        scratch_shapes=list(scratch),
        compiler_params=pltpu.CompilerParams(vmem_limit_bytes=VMEM_BYTES),
        cost_estimate=pl.CostEstimate(flops=flops, bytes_accessed=moved, transcendentals=0),
        name=name,
    )(place, *[far_array(x) for x in far], *near, *held)


def far_array(x):
    return pltpu.with_memory_space_constraint(x, pltpu.HBM)


def fetch(pairs, sems):
    copies = [pltpu.make_async_copy(src, dst, sems.at[i]) for i, (src, dst) in enumerate(pairs)]
    for copy in copies:
        copy.start()
    return copies


def deal(chip, core, shard, keep, give, value, first=0):
    rows = keep.shape[1]
    cols = slice(first, first + value.shape[1])
    mine = core == 0
    for i in range(0, value.shape[0], 2 * rows):
        even, odd = value[i : i + rows], value[i + rows : i + 2 * rows]
        slot = jnp.bitwise_xor(chip, (shard + i // rows) // 2)
        keep[slot, :, cols] = jnp.where(mine, even, odd)
        give[slot, :, cols] = jnp.where(mine, odd, even)


def scores(chip, core, left, right, keep, give, first):
    heads, _, cols = left.shape
    piece_rows = keep.shape[1]
    for h in range(heads):
        total = lax.dot_general(
            left[h], right[h], (((0,), (0,)), ((), ())), preferred_element_type=F32
        )
        deal(chip, core, h * cols // piece_rows, keep, give, total.astype(BF16), first)


def front_kernel(
    place, x, og, wq, wk, wv, wo, qt, kt, vt, gt, keep, give, slab,
    rows_x, rows_og, three_w, held_wo, both, sems,
):
    rows = x.shape[0]
    width = wq.shape[1]
    loads = [pltpu.make_async_copy(w, three_w.at[t], sems.at[2, t]) for t, w in enumerate((wq, wk, wv))]
    loads.append(pltpu.make_async_copy(wo, held_wo, sems.at[2, 3]))
    span = max(1, rows // 2)
    spans = [pl.ds(r, span) for r in range(0, rows, span)]
    in_x = [pltpu.make_async_copy(x.at[at], rows_x.at[at], sems.at[0, i]) for i, at in enumerate(spans)]
    in_og = [pltpu.make_async_copy(og, rows_og, sems.at[1, 0])]
    for copy in loads + in_x + in_og:
        copy.start()
    for copy in loads:
        copy.wait()
    depth = slab.shape[1]
    at = pl.ds(pl.multiple_of(place[3] * depth, depth), depth)
    for t in range(3):
        both[t * width : (t + 1) * width, :] = three_w[t].T
        slab[0, :, t * width : (t + 1) * width] = three_w[t, at, :]
    for r in range(rows):
        if r % span == 0:
            in_x[r // span].wait()
        three = dot_nt(both[...], rows_x[r]).astype(BF16)
        at = slice(r * HEAD_DIM, (r + 1) * HEAD_DIM)
        for t, out in enumerate((qt, kt, vt)):
            for h in range(width // HEAD_DIM):
                first = t * width + h * HEAD_DIM
                out[h, at, :] = three[first : first + HEAD_DIM]
    in_og[0].wait()
    for r in range(rows):
        grad = dot_nt(held_wo[...], rows_og[r]).astype(BF16)
        at = slice(r * HEAD_DIM, (r + 1) * HEAD_DIM)
        for h in range(width // HEAD_DIM):
            gt[h, at, :] = grad[h * HEAD_DIM : (h + 1) * HEAD_DIM]
    scores(place[0], place[1], qt, kt, keep, give, 0)
    scores(place[0], place[1], gt, vt, keep, give, kt.shape[2])


def pair_kernel(place, keep, got, *outs):
    for k in range(keep.shape[0]):
        outs[k][...] = (keep[k].astype(F32) + got[k].astype(F32)).astype(outs[k].dtype)


def join_kernel(place, *refs):
    *parts, out = refs
    at = 0
    for part in parts:
        out[at : at + part.shape[0]] = part[...]
        at += part.shape[0]


def pair_pass_kernel(place, keep, got, slab, *refs):
    *outs, passed = refs
    halves = len(outs) // keep.shape[0]
    rows = outs[0].shape[0]
    for k in range(keep.shape[0]):
        for j in range(halves):
            at = slice(j * rows, (j + 1) * rows)
            outs[k * halves + j][...] = (keep[k, at].astype(F32) + got[k, at].astype(F32)).astype(BF16)
    passed[...] = slab[...]


def pack_kernel(place, *refs):
    *slabs, out = refs
    at = 0
    for slab in slabs:
        count, depth, wide = slab.shape
        folds = out.shape[1] // wide
        rows = depth // folds
        for z in range(count):
            for i in range(folds):
                out[at : at + rows, i * wide : (i + 1) * wide] = slab[z, i * rows : (i + 1) * rows]
            at += rows


def added(parts, cols=slice(None)):
    total = parts[0][:, cols].astype(F32)
    for part in parts[1:]:
        total = total + part[:, cols].astype(F32)
    return total


def score_kernel(logit_scale, place, *refs):
    *parts, out = refs
    cols = out.shape[1] // 2
    exponent = jnp.exp(added(parts, slice(0, cols)) * logit_scale)
    probs = exponent / jnp.sum(exponent, axis=1, keepdims=True)
    out[:, 0:cols] = probs.astype(BF16)
    grad = added(parts, slice(cols, None))
    inner = jnp.sum(probs * grad, axis=1, keepdims=True)
    out[:, cols:] = (logit_scale * probs * (grad - inner)).astype(BF16)


def assemble(place, mine, other, full, halves=1, half=0):
    piece_rows = mine[0].shape[0]
    for k in range(len(mine)):
        base = 2 * jnp.bitwise_xor(place[0], k)
        for side, part in ((place[1], mine[k]), (1 - place[1], other[k])):
            first = ((base + side) * halves + half) * piece_rows
            at = pl.ds(pl.multiple_of(first, piece_rows), piece_rows)
            full[at, :] = part[0:piece_rows].astype(full.dtype)


def grads_kernel(pieces, halves, place, *refs):
    count = pieces * halves
    mine, other = refs[0:count], refs[count : 2 * count]
    qt, kt, vt, gt = refs[2 * count : 2 * count + 4]
    send_far, att_far, full, send, att, sems = refs[2 * count + 4 :]
    heads, _, cols = qt.shape
    zeds, width, tokens = att.shape
    block = cols // zeds
    for j in range(halves):
        each = slice(j * pieces, (j + 1) * pieces)
        assemble(place, mine[each], other[each], full, halves, j)
    copies = []
    for h in range(heads):
        span = slice(h * cols, (h + 1) * cols)
        values = (
            dot_nt(kt[h], full[span, cols:]),
            dot_nn(qt[h], full[span, cols:]),
            dot_nn(gt[h], full[span, 0:cols]),
            dot_nt(vt[h], full[span, 0:cols]),
        )
        for t, value in enumerate(values):
            value = value.astype(BF16)
            near, far, at = (send, send_far, t * width) if t < 3 else (att, att_far, 0)
            at = slice(at + h * HEAD_DIM, at + (h + 1) * HEAD_DIM)
            for r in range(tokens // block):
                part = value[r * HEAD_DIM : (r + 1) * HEAD_DIM]
                for z in range(zeds):
                    near[z, at, r * block : (r + 1) * block] = part[:, z * block : (z + 1) * block]
            copies += fetch([(near.at[:, at], far.at[:, at])], sems.at[pl.ds(h * 4 + t, 1)])
    for copy in copies:
        copy.wait()


def weights_kernel(place, x_far, og_far, send_far, att_far, keep, give, x, og, send, att, total, sems):
    zeds, three, tokens = send.shape
    rows, cols, model = x_far.shape
    block = cols // zeds
    stacked = total.shape[0]
    piece_rows = keep.shape[1]
    copies = []
    for z in range(zeds):
        at = pl.ds(z * block, block)
        pairs = [(send_far.at[z], send.at[z]), (x_far.at[:, at], x.at[z])]
        copies.append(fetch(pairs + [(att_far.at[z], att.at[z]), (og_far.at[:, at], og.at[z])], sems.at[z]))
    for z in range(zeds):
        for first, last, left, right, half in ((0, three, send, x, 0), (three, stacked, att, og, 2)):
            for copy in copies[z][half : half + 2]:
                copy.wait()
            part = dot_nn(left[z], right[z].reshape(tokens, model))
            if z > 0:
                part = part + total[first:last, :]
            if z < zeds - 1:
                total[first:last, :] = part
            else:
                deal(place[0], place[1], first // piece_rows, keep, give, part.astype(BF16))


def pair_append_kernel(place, keep, got, packed, *outs):
    pieces, piece_rows, _ = keep.shape
    for k in range(pieces):
        outs[k][0:piece_rows] = (keep[k].astype(F32) + got[k].astype(F32)).astype(BF16)
        if outs[k].shape[0] > piece_rows:
            outs[k][piece_rows:] = packed[...]


def sum_relay_kernel(scale, place, packed, *refs):
    *parts, out, first, second, third, slabs = refs
    rows, extra = out.shape[0], packed.shape[0]
    total = parts[0][0:rows].astype(F32)
    for part in parts[1:]:
        total = total + part[0:rows].astype(F32)
    total = (total * scale).astype(out.dtype)
    out[...] = total
    cut = first.shape[0] - rows
    for target in (first, second, third):
        target[0:rows] = total
    first[rows:] = parts[2][rows : rows + cut]
    second[rows:] = parts[1][rows + cut : rows + 2 * cut]
    third[rows:] = packed[2 * cut :]
    slabs[0] = parts[1][rows:]
    slabs[1] = parts[2][rows:]


def unpack_kernel(pieces, place, *refs):
    mine, other = refs[0:pieces], refs[pieces : 2 * pieces]
    outs, full = refs[2 * pieces : -1], refs[-1]
    assemble(place, mine, other, full)
    width = full.shape[0] // len(outs)
    for t, out in enumerate(outs[:-1]):
        out[...] = full[t * width : (t + 1) * width, :].T
    outs[-1][...] = full[(len(outs) - 1) * width :, :]


def gather_weights_kernel(zeds, place, own, own_other, near, near_other, *refs):
    *far, full = refs
    model = full.shape[0]
    wide = full.shape[1] // (zeds - 1)
    extra = own.shape[0]
    folds = model // wide
    rows = extra // (zeds - 1)
    depth = rows * folds
    cut = extra // 3 // 16 * 16
    skip = far[0].shape[0] - cut

    def part(side, k, first, count):
        if k == 0:
            return (own, own_other)[side][first : first + count]
        if k < 3:
            return (near, near_other)[side][k - 1, first : first + count]
        way = min(first // cut, 2)
        at = skip + first - way * cut
        return far[3 * side + way][at : at + count]

    unit = math.gcd(rows, cut)
    for k in range(4):
        base = 2 * jnp.bitwise_xor(place[3] // 2, k)
        for side, core in ((0, place[1]), (1, 1 - place[1])):
            for first in range(0, extra, unit):
                z, offset = 1 + first // rows, first % rows
                cols = slice((z - 1) * wide, z * wide)
                value = part(side, k, first, unit)
                for i in range(folds):
                    row = pl.multiple_of((base + core) * depth + i * rows + offset, unit)
                    full[pl.ds(row, unit), cols] = value[:, i * wide : (i + 1) * wide]


def own_inputs_kernel(place, send_far, wq, wk, wv, total, send, full, sems):
    width = wq.shape[1]
    pairs = [(w, full.at[:, t * width : (t + 1) * width]) for t, w in enumerate((wq, wk, wv))]
    for copy in fetch([(send_far.at[place[2]], send)] + pairs, sems):
        copy.wait()
    total[...] = dot_nn(full[...], send[...])


def inputs_kernel(place, sent_far, own_part, full, out_far, sent, out, sems):
    rows, block, _ = out.shape
    zeds, depth, _ = sent_far.shape
    pairs = []
    for k in range(1, zeds):
        far = sent_far.at[jnp.bitwise_xor(place[2], k)]
        pairs.append((far, sent.at[(k - 1) * depth : k * depth]))
    for copy in fetch(pairs, sems.at[0]):
        copy.wait()
    step = min(2, rows)
    copies = []
    for r in range(0, rows, step):
        span = slice(r * block, (r + step) * block)
        value = own_part[:, span] + dot_nn(full[...], sent[:, span])
        value = value.astype(BF16).T
        for i in range(step):
            out[r + i] = value[i * block : (i + 1) * block]
        here = pl.ds(r, step)
        copies += fetch([(out.at[here], out_far.at[here])], sems.at[1, pl.ds(r // step, 1)])
    for copy in copies:
        copy.wait()


def body(inputs, out_grad, w_query, w_key, w_value, w_output):
    rows, cols, model = inputs.shape
    width = w_query.shape[1]
    heads = width // HEAD_DIM
    merged = rows * HEAD_DIM
    seqs, zeds = lax.axis_size("seq"), lax.axis_size("head")
    pieces = seqs // 2
    all_rows = rows * seqs
    logit_scale = 1.0 / (math.sqrt(HEAD_DIM) * math.sqrt(all_rows))
    inv_root = 1.0 / math.sqrt(all_rows * cols)
    shard = heads * cols // seqs
    wide = 4 * width // seqs
    block = cols // zeds
    sharers = min(seqs, SHARERS)
    depth = model // sharers
    folds = model // (3 * width)
    me = lax.axis_index("seq")
    zed = lax.axis_index("head")
    place = jnp.stack([me // 2, me % 2, zed, me % sharers]).astype(jnp.int32)

    def swap(value):
        return lax.ppermute(value, "seq", [(i, i ^ 1) for i in range(seqs)])

    def across(value, k):
        return lax.ppermute(value, "seq", [(i, i ^ (2 * k)) for i in range(seqs)])

    def along(value, k):
        return lax.ppermute(value, "head", [(i, i ^ k) for i in range(zeds)])

    def shape(*dims, dtype=BF16):
        return jax.ShapeDtypeStruct(dims, dtype)

    def spread(paired):
        return [paired[0]] + [across(paired[k], k) for k in range(1, pieces)]

    def gathered(value, count):
        mine = [value] + [across(value, k) for k in range(1, count)]
        return mine, [swap(part) for part in mine]

    blocks = shape(heads, merged, cols)
    dealt = shape(pieces, shard, 2 * cols)
    rows_in = pltpu.VMEM((rows, cols, model), BF16)
    dot_flops = 2 * rows * cols * width * model
    score_flops = 2 * heads * cols * cols * merged

    qt, kt, vt, gt, keep, give, slab = call(
        front_kernel,
        (blocks,) * 4 + (dealt,) * 2 + (shape(1, depth, 3 * width),),
        (place, inputs, out_grad, w_query, w_key, w_value, w_output),
        hbm=6,
        scratch=[
            rows_in,
            rows_in,
            pltpu.VMEM((3, model, width), BF16),
            pltpu.VMEM((width, model), BF16),
            pltpu.VMEM((3 * width, model), BF16),
            pltpu.SemaphoreType.DMA((3, max(4, rows))),
        ],
        flops=4 * dot_flops + 2 * score_flops,
        name="front",
    )
    halves = 2 if shard % 32 == 0 else 1
    *paired, slab = call(
        pair_pass_kernel,
        [shape(shard // halves, 2 * cols)] * (pieces * halves) + [shape(*slab.shape)],
        (place, keep, swap(give), slab),
        name="pair_scores",
    )
    parts = [spread(paired[j::halves]) for j in range(halves)]
    groups, span = [slab], 1
    while span < zeds:
        if span > 1:
            slab = call(join_kernel, shape(span, depth, 3 * width), (place, *groups), name="join")
        groups.append(along(slab, span))
        span *= 2
    mine, other = [], []
    for j in range(halves):
        scored = call(
            partial(score_kernel, logit_scale),
            shape(shard // halves, 2 * cols),
            (place, *parts[j]),
            held=(slab,) if j == 9 else (),
            name="score",
        )
        near, far = gathered(scored, pieces)
        mine += near
        other += far
    swapped = [swap(group) for group in groups[1:]]
    send, att = call(
        partial(grads_kernel, pieces, halves),
        (
            pltpu.HBM((zeds, 3 * width, rows * block), BF16),
            pltpu.HBM((zeds, width, rows * block), BF16),
        ),
        (place, *mine, *other, qt, kt, vt, gt),
        held=groups[1:],
        out_specs=(hbm_spec(), hbm_spec()),
        scratch=[
            pltpu.VMEM((heads * cols, 2 * cols), BF16),
            pltpu.VMEM((zeds, 3 * width, rows * block), BF16),
            pltpu.VMEM((zeds, width, rows * block), BF16),
            pltpu.SemaphoreType.DMA((heads * 4,)),
        ],
        flops=4 * score_flops,
        name="grads",
    )
    own_part = call(
        own_inputs_kernel,
        shape(model, rows * block, dtype=F32),
        (place, send, w_query, w_key, w_value),
        hbm=4,
        scratch=[
            pltpu.VMEM((3 * width, rows * block), BF16),
            pltpu.VMEM((model, 3 * width), BF16),
            pltpu.SemaphoreType.DMA((4,)),
        ],
        flops=3 * dot_flops // zeds,
        name="own_inputs",
    )
    sent = lax.all_to_all(send, "head", 0, 0, tiled=True)

    keep, give = call(
        weights_kernel,
        [shape(pieces, wide, model)] * 2,
        (place, inputs, out_grad, send, att),
        hbm=4,
        scratch=[
            pltpu.VMEM((zeds, rows, block, model), BF16),
            pltpu.VMEM((zeds, rows, block, model), BF16),
            pltpu.VMEM((zeds, 3 * width, rows * block), BF16),
            pltpu.VMEM((zeds, width, rows * block), BF16),
            pltpu.VMEM((4 * width, model), F32),
            pltpu.SemaphoreType.DMA((zeds, 4)),
        ],
        flops=4 * dot_flops,
        moved=inputs.size * 4,
        name="weights",
    )
    packed, packed_other = [
        call(pack_kernel, shape((zeds - 1) * depth // folds, model), (place, *parts), name="pack")
        for parts in (groups[1:], swapped)
    ]
    extra = packed.shape[0]
    cut = extra // 48 * 16
    near = (1, 2)
    paired = call(
        pair_append_kernel,
        [shape(wide + (extra if k in near else 0), model) for k in range(pieces)],
        (place, keep, swap(give), packed),
        name="pair_weights",
    )
    parts = spread(paired)
    total_w, first, second, third, slabs = call(
        partial(sum_relay_kernel, inv_root),
        (
            shape(wide, model),
            shape(wide + cut, model),
            shape(wide + cut, model),
            shape(wide + extra - 2 * cut, model),
            shape(2, extra, model),
        ),
        (place, packed, *parts),
        held=(own_part,),
        name="sum_weights",
    )
    sums = [total_w, first, second, third] + [total_w] * (pieces - 4)
    mine = [total_w] + [across(sums[k], k) for k in range(1, pieces)]
    other = [swap(part) for part in mine]
    full = call(
        partial(gather_weights_kernel, zeds),
        shape(model, (zeds - 1) * 3 * width),
        (place, packed, packed_other, slabs, swap(slabs))
        + (*mine[1:4], *other[1:4]),
        name="gather_weights",
    )
    grad_q, grad_k, grad_v, grad_o = call(
        partial(unpack_kernel, pieces),
        [shape(model, width, dtype=F32)] * 3 + [shape(width, model, dtype=F32)],
        (place, *mine, *other),
        scratch=[pltpu.VMEM((4 * width, model), F32)],
        name="unpack",
    )
    grad_inputs = call(
        inputs_kernel,
        pltpu.HBM((rows, block, model), BF16),
        (place, sent, own_part, full),
        hbm=1,
        scratch=[
            pltpu.VMEM(((zeds - 1) * 3 * width, rows * block), BF16),
            pltpu.VMEM((rows, block, model), BF16),
            pltpu.SemaphoreType.DMA((2, max(zeds, rows))),
        ],
        out_specs=hbm_spec(),
        flops=3 * dot_flops * (zeds - 1) // zeds,
        name="inputs",
    )
    return (grad_inputs, grad_q, grad_k, grad_v, grad_o)


def solution(mesh):
    return jax.shard_map(
        body,
        mesh=mesh,
        in_specs=(
            P("seq", None, None),
            P("seq", None, None),
            P(None, "head"),
            P(None, "head"),
            P(None, "head"),
            P("head", None),
        ),
        out_specs=(
            P("seq", "head", None),
            P(None, "head"),
            P(None, "head"),
            P(None, "head"),
            P("head", None),
        ),
        check_vma=False,
    )
```
